256 devices in a mesh: dp: 16 (over z_lo, x), tensor: 16 (over y, z_hi, core).
Axes of the slice: x: 4, y: 4, z: 8 (z_hi: 2, z_lo: 4; z = z_hi * 4 + z_lo), core: 2. Of those that a mesh axis runs over, the one named last changes fastest.
Arguments:
- queries: bfloat16 [4096, 6144], P('dp', 'tensor'), may hold values from -28 to 28
- key_rows: bfloat16 [4096, 6144], P('dp', 'tensor'), may hold values from -4 to 4
- value_rows: bfloat16 [4096, 6144], P('dp', 'tensor'), may hold values from -6 to 6
- residual_in: bfloat16 [4096, 12288], P(('dp', 'tensor')), may hold values from -3 to 3
- out_weight: bfloat16 [12288, 6144], P('dp', 'tensor'), may hold values from -0.25 to 0.25
- encoder: bfloat16 [96, 32, 128], replicated, may hold values from -0.5 to 0.5
- decoder: bfloat16 [96, 32, 128], replicated, may hold values from -1 to 1
- grad_out: bfloat16 [4096, 12288], P(('dp', 'tensor')), may hold values from -2.5 to 2.5
Outputs:
- layer_out: bfloat16 [4096, 12288], P('dp')
- grad_queries: bfloat16 [4096, 6144], P('dp', 'tensor')
- grad_keys: bfloat16 [4096, 6144], P('dp', 'tensor')
- grad_values: bfloat16 [4096, 6144], P('dp', 'tensor')
- grad_weight: float32 [12288, 6144], P('dp', 'tensor')
The draws below stay inside these ranges and needn't reach their ends.
All inputs are finite; a program needn't handle non-finite values.
Results may differ from the reference program's by a relative error of at most 0.022.
Values may be sent and summed in bfloat16 or wider, within the bound.
A program may use at most 128 MiB of HBM per device.

```python
import math
import jax
import jax.numpy as jnp
from jax import lax

D = 12288
HEADS = 48
HD = 128
BLOCK = 128
CODE_W = 32
SEQ = 256
ATTN_W = 6144
NBLK = 96
CODE = 3072
TOKENS = 4096
N_TENSOR = 16


def draw_key_rows(key, part):
    key = jax.random.fold_in(key, 7)
    shape = (TOKENS // SEQ, SEQ, HEADS * HD)
    drawn = jnp.clip(1.4 * jax.random.normal(key, shape, jnp.float32), -4.0, 4.0)
    return drawn.reshape(TOKENS, HEADS * HD).astype(jnp.bfloat16)


def draw_queries(key, part):
    key = jax.random.fold_in(key, 5)
    shape = (TOKENS // SEQ, SEQ, HEADS * HD)
    drawn = jnp.clip(1.4 * jax.random.normal(key, shape, jnp.float32), -4.0, 4.0)
    return drawn.reshape(TOKENS, HEADS * HD).astype(jnp.bfloat16)


def strengthened(entries, key, source, target, blocks, factor):
    def block_of(axis_at):
        return (jnp.arange(entries.shape[axis_at]) // (entries.shape[axis_at] // blocks)).reshape((-1,) + (1,) * (entries.ndim - 1 - axis_at))

    first = jax.random.permutation(key, blocks)[block_of(target)]
    far = (block_of(target) + blocks // 2) % blocks
    return jnp.where((block_of(source) == first) | (block_of(source) == far), factor * entries, entries)


def levels(key, shape, shards, smallest, largest):
    loudness, own = 1.0, jax.random.fold_in(key, 6)
    for position, blocks in shards:
        heights = jnp.exp(jax.random.uniform(jax.random.fold_in(own, position), (blocks,), jnp.float32, smallest / len(shards), largest / len(shards)))
        loudness = loudness * jnp.repeat(heights, shape[position] // blocks).reshape([-1 if axis == position else 1 for axis in range(len(shape))])
    return loudness


def centred(rng, dims, scale, reach, split=(), held_as=jnp.bfloat16):
    result = jax.random.normal(rng, dims, jnp.float32) * scale
    if len(split) > 0:
        result = levels(rng, dims, split, -0.22, 0.18) * result
    return jnp.clip(result, min=-reach, max=reach).astype(held_as)


def bell_draw_with(key, extent, deviation, most, pieces, heavy, kind=jnp.bfloat16):
    values = deviation * jax.random.normal(key, extent, jnp.float32)
    if pieces:
        values = values * levels(key, extent, pieces, -0.22, 0.18)
    return jnp.clip(strengthened(values, jax.random.fold_in(key, 3), *heavy), -most, most).astype(kind)


def setup_inputs(seed: int = 0) -> dict:
    key_of = jax.random.split(jax.random.key(seed), 9)
    queries = draw_queries(jax.random.fold_in(key_of[8], 71), 0)
    key_rows = draw_key_rows(jax.random.fold_in(key_of[8], 71), 0)
    value_rows = centred(key_of[2], (TOKENS, ATTN_W), 1.0, 6.0, ((0, 16), (1, 16)))
    residual_in = centred(key_of[3], (TOKENS, D), 0.5, 3.0, ((0, 256),))
    out_weight = centred(key_of[4], (D, ATTN_W), (4 * HD) ** -0.5, 0.25, ((0, 16), (1, 16)))
    encoder = centred(key_of[5], (NBLK, CODE_W, BLOCK), BLOCK ** -0.5, 0.5)
    decoder = centred(key_of[6], (NBLK, CODE_W, BLOCK), CODE_W ** -0.5, 1.0)
    grad_out = bell_draw_with(key_of[7], (TOKENS, D), 0.1, 2.5, ((0, 256),), (0, 1, 256, 6.0))
    return {"queries": queries, "key_rows": key_rows, "value_rows": value_rows, "residual_in": residual_in, "out_weight": out_weight, "encoder": encoder, "decoder": decoder, "grad_out": grad_out}


NEG_FILL = -1e+30
HIGH = lax.Precision.HIGHEST

def split_heads(matrix, head_size):
    return matrix.reshape(matrix.shape[0], matrix.shape[1] // head_size, head_size).astype(jnp.float32)

def causal_probs(query_heads, key_heads):
    length = query_heads.shape[0]
    score_scale = 1.0 / math.sqrt(query_heads.shape[2])
    scores = jnp.einsum('qhd,khd->hqk', query_heads, key_heads, precision=HIGH) * score_scale
    row_index = lax.broadcasted_iota(jnp.int32, (length, length), 0)
    col_index = lax.broadcasted_iota(jnp.int32, (length, length), 1)
    scores = jnp.where(col_index <= row_index, scores, NEG_FILL)
    row_max = lax.optimization_barrier(jnp.max(scores, axis=-1, keepdims=True))
    weights = jnp.exp(scores - row_max)
    return weights / lax.optimization_barrier(jnp.sum(weights, axis=-1, keepdims=True))

def attend_forward(queries, key_rows, value_rows, head_size):
    probs = causal_probs(split_heads(queries, head_size), split_heads(key_rows, head_size))
    probs_bf = probs.astype(jnp.bfloat16).astype(jnp.float32)
    mixed = jnp.einsum('hqk,khd->qhd', probs_bf, split_heads(value_rows, head_size), precision=HIGH)
    return mixed.astype(jnp.bfloat16).reshape(queries.shape)

def attend_backward(queries, key_rows, value_rows, grad_attn, head_size):
    query_heads = split_heads(queries, head_size)
    key_heads = split_heads(key_rows, head_size)
    value_heads = split_heads(value_rows, head_size)
    grad_heads = split_heads(grad_attn, head_size)
    probs = causal_probs(query_heads, key_heads)
    probs_bf = probs.astype(jnp.bfloat16).astype(jnp.float32)
    dprobs = jnp.einsum('qhd,khd->hqk', grad_heads, value_heads, precision=HIGH)
    center = lax.optimization_barrier(jnp.sum(dprobs * probs, axis=-1, keepdims=True))
    grad_scores = (probs * (dprobs - center) * (1.0 / math.sqrt(head_size))).astype(jnp.bfloat16).astype(jnp.float32)
    grad_query = jnp.einsum('hqk,khd->qhd', grad_scores, key_heads, precision=HIGH)
    grad_key = jnp.einsum('hqk,qhd->khd', grad_scores, query_heads, precision=HIGH)
    grad_value = jnp.einsum('hqk,qhd->khd', probs_bf, grad_heads, precision=HIGH)
    shape = queries.shape
    return (grad_query.astype(jnp.bfloat16).reshape(shape), grad_key.astype(jnp.bfloat16).reshape(shape), grad_value.astype(jnp.bfloat16).reshape(shape))

def encode(partial_value, encoder):
    count = partial_value.shape[0]
    block_count, code_width, block_size = encoder.shape
    blocks = partial_value.reshape(count, block_count, block_size)
    coded = jnp.einsum('nbk,bck->nbc', blocks, encoder.astype(jnp.float32), precision=HIGH)
    return coded.reshape(count, block_count * code_width)

def decode(code_sum, decoder):
    count = code_sum.shape[0]
    block_count, code_width, block_size = decoder.shape
    blocks = code_sum.reshape(count, block_count, code_width)
    opened = jnp.einsum('nbc,bck->nbk', blocks, decoder.astype(jnp.float32), precision=HIGH)
    return opened.reshape(count, block_count * block_size)

def code_grad(grad_rows, decoder):
    count = grad_rows.shape[0]
    block_count, code_width, block_size = decoder.shape
    blocks = grad_rows.reshape(count, block_count, block_size).astype(jnp.float32)
    coded = jnp.einsum('nbk,bck->nbc', blocks, decoder.astype(jnp.float32), precision=HIGH)
    return coded.reshape(count, block_count * code_width).astype(jnp.bfloat16)

def expand(grad_codes, encoder):
    count = grad_codes.shape[0]
    block_count, code_width, block_size = encoder.shape
    blocks = grad_codes.reshape(count, block_count, code_width).astype(jnp.float32)
    opened = jnp.einsum('nbc,bck->nbk', blocks, encoder.astype(jnp.float32), precision=HIGH)
    return opened.reshape(count, block_count * block_size).astype(jnp.bfloat16)

def reference(queries, key_rows, value_rows, residual_in, out_weight, encoder, decoder, grad_out):
    seq_count = TOKENS // SEQ
    attn_width = HEADS * HD
    local_width = attn_width // N_TENSOR
    inputs = (queries.reshape(seq_count, SEQ, attn_width), key_rows.reshape(seq_count, SEQ, attn_width), value_rows.reshape(seq_count, SEQ, attn_width), residual_in.reshape(seq_count, SEQ, D), grad_out.reshape(seq_count, SEQ, D))

    def per_sequence(grad_weight, parts):
        query_seq, key_seq, value_seq, resid_seq, grad_seq = parts
        attn_out = attend_forward(query_seq, key_seq, value_seq, HD)

        def group_step(running, group_index):
            offset = (group_index * local_width).astype(jnp.int32)
            picked = lax.dynamic_slice_in_dim(attn_out, offset, local_width, 1)
            columns = lax.dynamic_slice_in_dim(out_weight, offset, local_width, 1)
            partial_value = jnp.dot(picked, columns.T, preferred_element_type=jnp.float32)
            code_term = encode(partial_value, encoder).astype(jnp.bfloat16)
            return (running + code_term.astype(jnp.float32), None)
        code_sum, _ = lax.scan(group_step, jnp.zeros((SEQ, CODE), jnp.float32), jnp.arange(N_TENSOR, dtype=jnp.int32))
        layer = (resid_seq.astype(jnp.float32) + decode(code_sum, decoder)).astype(jnp.bfloat16)
        grad_codes = code_grad(grad_seq, decoder)
        grad_partial = expand(grad_codes, encoder)
        grad_attn = jnp.dot(grad_partial, out_weight, preferred_element_type=jnp.float32).astype(jnp.bfloat16)
        grad_weight = grad_weight + jnp.dot(grad_partial.T, attn_out, preferred_element_type=jnp.float32)
        grad_query, grad_key, grad_value = attend_backward(query_seq, key_seq, value_seq, grad_attn, HD)
        return (grad_weight, (layer, grad_query, grad_key, grad_value))
    grad_weight, stacked = lax.scan(per_sequence, jnp.zeros((D, attn_width), jnp.float32), inputs)
    layer_out = stacked[0].reshape(TOKENS, D)
    grad_queries = stacked[1].reshape(TOKENS, attn_width)
    grad_keys = stacked[2].reshape(TOKENS, attn_width)
    grad_values = stacked[3].reshape(TOKENS, attn_width)
    return (layer_out, grad_queries, grad_keys, grad_values, grad_weight)
```

```python
import math

import jax
import jax.numpy as jnp
from jax import lax
from jax.sharding import PartitionSpec as P

HD = 128


NEG_FILL = -1e30


def split_heads(matrix, head_size):
    return matrix.reshape(matrix.shape[0], matrix.shape[1] // head_size, head_size)


def causal_probs(query_heads, key_heads):
    length = query_heads.shape[0]
    score_scale = 1.0 / math.sqrt(query_heads.shape[2])
    scores = (
        jnp.einsum("qhd,khd->hqk", query_heads, key_heads, preferred_element_type=jnp.float32)
        * score_scale
    )
    row_index = lax.broadcasted_iota(jnp.int32, (length, length), 0)
    col_index = lax.broadcasted_iota(jnp.int32, (length, length), 1)
    scores = jnp.where(col_index <= row_index, scores, NEG_FILL)
    row_max = jnp.max(scores, axis=-1, keepdims=True)
    weights = jnp.exp(scores - row_max)
    return weights / jnp.sum(weights, axis=-1, keepdims=True)


def attend_forward(queries, key_rows, value_rows, head_size):
    probs = causal_probs(split_heads(queries, head_size), split_heads(key_rows, head_size))
    probs_bf = probs.astype(jnp.bfloat16)
    mixed = jnp.einsum(
        "hqk,khd->qhd",
        probs_bf,
        split_heads(value_rows, head_size),
        preferred_element_type=jnp.float32,
    )
    return mixed.astype(jnp.bfloat16).reshape(queries.shape)


def attend_backward(queries, key_rows, value_rows, grad_attn, head_size):
    query_heads = split_heads(queries, head_size)
    key_heads = split_heads(key_rows, head_size)
    value_heads = split_heads(value_rows, head_size)
    grad_heads = split_heads(grad_attn, head_size)
    probs = causal_probs(query_heads, key_heads)
    probs_bf = probs.astype(jnp.bfloat16)
    dprobs = jnp.einsum("qhd,khd->hqk", grad_heads, value_heads, preferred_element_type=jnp.float32)
    center = jnp.sum(dprobs * probs, axis=-1, keepdims=True)
    grad_scores = (probs * (dprobs - center) * (1.0 / math.sqrt(head_size))).astype(jnp.bfloat16)
    grad_query = jnp.einsum(
        "hqk,khd->qhd", grad_scores, key_heads, preferred_element_type=jnp.float32
    )
    grad_key = jnp.einsum(
        "hqk,qhd->khd", grad_scores, query_heads, preferred_element_type=jnp.float32
    )
    grad_value = jnp.einsum(
        "hqk,qhd->khd", probs_bf, grad_heads, preferred_element_type=jnp.float32
    )
    shape = queries.shape
    return (
        grad_query.astype(jnp.bfloat16).reshape(shape),
        grad_key.astype(jnp.bfloat16).reshape(shape),
        grad_value.astype(jnp.bfloat16).reshape(shape),
    )


def fold_weight(weight_rows, encoder_rows):
    blocks = weight_rows.reshape(encoder_rows.shape[0], encoder_rows.shape[2], weight_rows.shape[1])
    folded = jnp.einsum("bck,bkh->bch", encoder_rows, blocks, preferred_element_type=jnp.float32)
    return folded.reshape(-1, weight_rows.shape[1]).astype(jnp.bfloat16)


def decode(code_sum, decoder):
    count = code_sum.shape[0]
    block_count, code_width, block_size = decoder.shape
    blocks = code_sum.reshape(count, block_count, code_width)
    opened = jnp.einsum("nbc,bck->nbk", blocks, decoder, preferred_element_type=jnp.float32)
    return opened.reshape(count, block_count * block_size)


def code_grad(grad_rows, decoder):
    count = grad_rows.shape[0]
    block_count, code_width, block_size = decoder.shape
    blocks = grad_rows.reshape(count, block_count, block_size)
    coded = jnp.einsum("nbk,bck->nbc", blocks, decoder, preferred_element_type=jnp.float32)
    return coded.reshape(count, block_count * code_width).astype(jnp.bfloat16)


def local(queries, key_rows, value_rows, residual_in, out_weight, encoder, decoder, grad_out):
    block_count, code_width, block_size = encoder.shape
    own_blocks = out_weight.shape[0] // block_size
    encoder_rows = lax.dynamic_slice_in_dim(
        encoder, lax.axis_index("dp") * own_blocks, own_blocks, 0
    )
    folded = lax.all_gather(fold_weight(out_weight, encoder_rows), "dp", axis=0, tiled=True)
    grad_codes = lax.all_gather(code_grad(grad_out, decoder), "tensor", axis=0, tiled=True)
    residual = lax.all_gather(residual_in, "tensor", axis=0, tiled=True)
    attn_out = attend_forward(queries, key_rows, value_rows, HD)
    codes = lax.dot_general(
        attn_out, folded, (((1,), (1,)), ((), ())), preferred_element_type=jnp.float32
    ).astype(jnp.bfloat16)
    code_rows = lax.psum_scatter(codes, "tensor", scatter_dimension=0, tiled=True)
    code_sum = lax.all_gather(code_rows, "tensor", axis=0, tiled=True)
    grad_attn_rows = jnp.dot(grad_codes, folded, preferred_element_type=jnp.float32).astype(
        jnp.bfloat16
    )
    code_weight = lax.psum_scatter(
        lax.dot_general(
            grad_codes, attn_out, (((0,), (0,)), ((), ())), preferred_element_type=jnp.float32
        ).astype(jnp.bfloat16),
        "dp",
        scatter_dimension=0,
        tiled=True,
    )
    grad_weight = jnp.einsum(
        "bck,bch->bkh",
        encoder_rows,
        code_weight.reshape(own_blocks, code_width, -1),
        preferred_element_type=jnp.float32,
    ).reshape(out_weight.shape)
    grad_query, grad_key, grad_value = attend_backward(
        queries, key_rows, value_rows, grad_attn_rows, HD
    )
    layer_out = (residual.astype(jnp.float32) + decode(code_sum, decoder)).astype(jnp.bfloat16)
    return (layer_out, grad_query, grad_key, grad_value, grad_weight)


def solution(mesh):
    placed = (
        P("dp", "tensor"),
        P("dp", "tensor"),
        P("dp", "tensor"),
        P(("dp", "tensor"), None),
        P("dp", "tensor"),
        P(),
        P(),
        P(("dp", "tensor"), None),
    )
    return jax.shard_map(
        local,
        mesh=mesh,
        in_specs=placed,
        out_specs=(
            P("dp", None),
            P("dp", "tensor"),
            P("dp", "tensor"),
            P("dp", "tensor"),
            P("dp", "tensor"),
        ),
        check_vma=False,
    )
```

```python
import math

import jax
import jax.numpy as jnp
from jax import lax
from jax.experimental import pallas as pl
from jax.experimental.pallas import tpu as pltpu
from jax.sharding import PartitionSpec as P

HD = 128
NEG_FILL = -1e30
MESH = pl.DeviceIdType.MESH
BF, F32 = jnp.bfloat16, jnp.float32

NX, NZL, NY, NZH, NC = 4, 4, 4, 2, 2
TB = 16
SEQ = 256
HEADS = 3
AW = HEADS * HD
NBLK, CODE_W, BLOCK = 96, 32, 128
CODE = NBLK * CODE_W
D = NBLK * BLOCK
OWN = 6
ER = OWN * CODE_W
CH = NX * ER
HALF = SEQ // NC
PAIR = TB * NZH


def nt(a, b):
    return lax.dot_general(a, b, (((1,), (1,)), ((), ())), preferred_element_type=F32)


def nn(a, b):
    return lax.dot_general(a, b, (((1,), (0,)), ((), ())), preferred_element_type=F32)


def tn(a, b):
    return lax.dot_general(a, b, (((0,), (0,)), ((), ())), preferred_element_type=F32)


def place(t):
    return ((t % NC) * NY + t // (NC * NZH)) * NZH + (t // NC) % NZH


class Sems:
    def __init__(self, send, recv):
        self.send, self.recv, self.used, self.started = send, recv, 0, []

    def copy(self, src, dst, target):
        i = self.used
        self.used += 1
        made = pltpu.make_async_remote_copy(
            src_ref=src,
            dst_ref=dst,
            send_sem=self.send.at[i],
            recv_sem=self.recv.at[i],
            device_id=target,
            device_id_type=MESH,
        )
        made.start()
        self.started.append(made)
        return made


N_SEMS = 160


def main_kernel(
    q_ref, k_ref, v_ref, res_ref, w_ref, enc_ref, dec_ref, go_ref,
    resid_ref, cs_ref, dq_ref, dk_ref, dv_ref, gw_ref,
    ew, gcb, attn_p, probs, ga, enc,
    c_own, c_send, c_recv, y_sum, y_recv, z_sum, z_recv, ag,
    gp, gx_recv, gx_sum, gz_recv,
    send_sem, recv_sem, local_sem,
):
    dp, t = lax.axis_index("dp"), lax.axis_index("tensor")
    zl, x = dp // NX, dp % NX
    y, zh, c = t // (NZH * NC), (t // NC) % NZH, t % NC

    def to_x(k):
        return (zl * NX + (x + k) % NX, t)

    def to_zl(k):
        return (((zl + k) % NZL) * NX + x, t)

    def to_y(k):
        return (dp, (((y + k) % NY) * NZH + zh) * NC + c)

    to_zh = (dp, (y * NZH + 1 - zh) * NC + c)
    to_c = (dp, (y * NZH + zh) * NC + 1 - c)
    steps = (1, 3, 2)

    sems = Sems(send_sem, recv_sem)
    send = sems.copy

    barrier = pltpu.get_barrier_semaphore()
    peers = [to_x(k) for k in steps] + [to_zl(k) for k in steps]
    peers += [to_y(k) for k in steps] + [to_zh, to_c]
    for peer in peers:
        pl.semaphore_signal(barrier, inc=1, device_id=peer, device_id_type=MESH)

    enc_copy = pltpu.make_async_copy(
        enc_ref.at[pl.ds(dp * OWN, OWN)], enc, local_sem.at[0]
    )
    enc_copy.start()
    own_rows = pl.ds(pl.multiple_of(t * TB, TB), TB)
    own_res = pltpu.make_async_copy(res_ref, resid_ref.at[own_rows], local_sem.at[1])
    own_res.start()

    enc_copy.wait()
    for b in range(OWN):
        rows = pl.ds(pl.multiple_of(x * ER + b * CODE_W, CODE_W), CODE_W)
        ew[zl, rows, :] = nn(enc[b], w_ref[b * BLOCK : (b + 1) * BLOCK, :]).astype(BF)

    def place_of(y_, zh_, c_):
        return (c_ * NY + y_) * NZH + zh_

    def block_rows(p, n=1):
        return pl.ds(pl.multiple_of(p * TB, TB), TB * n)

    mine = block_rows(place_of(y, zh, c))
    lane_block = lax.broadcasted_iota(jnp.int32, (TB, BLOCK), 1) // CODE_W
    for g in range(NBLK // 4):
        wide = jnp.concatenate(
            [go_ref[:, (4 * g + j) * BLOCK : (4 * g + j + 1) * BLOCK] for j in range(4)], axis=0
        )
        coded = nt(wide, dec_ref[g * BLOCK : (g + 1) * BLOCK, :])
        picked = coded[:TB]
        for j in range(1, 4):
            picked = jnp.where(lane_block == j, coded[j * TB : (j + 1) * TB], picked)
        gcb[g // 6, mine, (g % 6) * BLOCK : (g % 6 + 1) * BLOCK] = picked.astype(BF)

    pl.semaphore_wait(barrier, len(peers))

    def ew_at(zl_, x_):
        return ew.at[zl_, pl.ds(pl.multiple_of(x_ * ER, ER), ER)]

    gc_z = send(gcb.at[:, mine], gcb.at[:, mine], to_zh)
    gc_y = {}
    for k in steps:
        gc_y[k, 0] = send(gcb.at[:, mine], gcb.at[:, mine], to_y(k))
    ew_z = {k: send(ew_at(zl, x), ew_at(zl, x), to_zl(k)) for k in steps}
    ew_x = {}
    for k in steps:
        ew_x[0, k] = send(ew_at(zl, x), ew_at(zl, x), to_x(k))

    row_index = lax.broadcasted_iota(jnp.int32, (SEQ, SEQ), 0)
    col_index = lax.broadcasted_iota(jnp.int32, (SEQ, SEQ), 1)
    scale = 1.0 / math.sqrt(HD)
    for h in range(HEADS):
        cols = slice(h * HD, (h + 1) * HD)
        scores = nt(q_ref[:, cols], k_ref[:, cols]) * scale
        scores = jnp.where(col_index <= row_index, scores, NEG_FILL)
        weights = jnp.exp(scores - jnp.max(scores, axis=-1, keepdims=True))
        prob = weights / jnp.sum(weights, axis=-1, keepdims=True)
        probs[h] = prob
        mixed = nn(prob.astype(BF), v_ref[:, cols]).astype(BF)
        for b in range(SEQ // TB):
            p = place(b)
            attn_p[p * TB : (p + 1) * TB, cols] = mixed[b * TB : (b + 1) * TB]

    gc_z.wait_recv()
    other = block_rows(place_of(y, 1 - zh, c))
    for k in steps:
        gc_y[k, 1] = send(gcb.at[:, other], gcb.at[:, other], to_y(k))
    pair = block_rows(place_of(y, 0, c), NZH)
    gc_c = [send(gcb.at[:, pair], gcb.at[:, pair], to_c)]
    order = (0,) + steps
    for k in steps:
        ew_z[k].wait_recv()
        from_zl = (zl - k + NZL) % NZL
        for j in steps:
            ew_x[k, j] = send(ew_at(from_zl, x), ew_at(from_zl, x), to_x(j))
    for k in steps:
        gc_y[k, 0].wait_recv()
        gc_y[k, 1].wait_recv()
        pair = block_rows(place_of((y - k + NY) % NY, 0, c), NZH)
        gc_c.append(send(gcb.at[:, pair], gcb.at[:, pair], to_c))
    for made in gc_c:
        made.wait_recv()

    def res_at(y_, zh_):
        return resid_ref.at[pl.ds(pl.multiple_of((y_ * NZH + zh_) * (NC * TB) + c * TB, TB), TB)]

    res_z = send(res_ref, res_at(y, zh), to_zh)
    res_y = {}
    for k in steps:
        res_y[k, 0] = send(res_ref, res_at(y, zh), to_y(k))

    for z_ in range(NZL):
        term = tn(gcb[z_], attn_p[...])
        for x_ in range(NX):
            gp[x_, z_] = term[x_ * ER : (x_ + 1) * ER].astype(BF)
    gx = {}
    for k in steps:
        gx[k] = send(gp.at[(x + k) % NX], gx_recv.at[k - 1], to_x(k))

    zls = [(zl - k + NZL) % NZL for k in order]
    c_cp, y_cp, z_cp, a_cp, ac_cp = {}, {}, {}, {}, {}

    def stage_code(i):
        k, z_ = order[i], zls[i]
        for j in steps:
            ew_x[k, j].wait_recv()
        codes = nt(attn_p[...], ew[z_]).astype(BF)
        for half in range(NC):
            part = codes[half * HALF : (half + 1) * HALF]

            @pl.when(c == half)
            def _():
                c_own[i] = part

            @pl.when(c != half)
            def _():
                c_send[i] = part

        c_cp[i] = send(c_send.at[i], c_recv.at[i], to_c)
        grown = nn(gcb[z_], ew[z_])
        if i == 0:
            ga[...] = grown
        else:
            ga[...] += grown

    def stage_core(i):
        c_cp[i].wait_recv()
        y_sum[i] = (c_own[i].astype(F32) + c_recv[i].astype(F32)).astype(BF)
        for k in steps:
            rows = pl.ds(pl.multiple_of(((y + k) % NY) * PAIR, PAIR), PAIR)
            y_cp[i, k] = send(y_sum.at[i, rows], y_recv.at[i, k - 1], to_y(k))

    def stage_y(i):
        for k in steps:
            y_cp[i, k].wait_recv()
        rows = pl.ds(pl.multiple_of(y * PAIR, PAIR), PAIR)
        total = y_sum[i, rows].astype(F32)
        for k in range(3):
            total += y_recv[i, k].astype(F32)
        z_sum[i] = total.astype(BF)
        z_cp[i] = send(z_sum.at[i], z_recv.at[i], to_zh)

    def ag_rows(y_):
        return pl.ds(pl.multiple_of((c * NY + y_) * PAIR, PAIR), PAIR)

    def stage_z(i):
        z_cp[i].wait_recv()
        z_ = zls[i]
        rows = ag_rows(y)
        ag[z_, rows] = (z_sum[i].astype(F32) + z_recv[i].astype(F32)).astype(BF)
        for k in steps:
            a_cp[i, k] = send(ag.at[z_, rows], ag.at[z_, rows], to_y(k))
        ac_cp[i, 0] = send(ag.at[z_, rows], ag.at[z_, rows], to_c)

    def stage_out(i):
        z_ = zls[i]
        for k in steps:
            a_cp[i, k].wait_recv()
            rows = ag_rows((y - k + NY) % NY)
            ac_cp[i, k] = send(ag.at[z_, rows], ag.at[z_, rows], to_c)

    def stage_done(i):
        for k in order:
            ac_cp[i, k].wait_recv()
        copy = pltpu.make_async_copy(ag.at[zls[i]], cs_ref.at[zls[i]], local_sem.at[2 + i])
        copy.start()
        return copy

    def attention_backward():
        for h in range(HEADS):
            cols = slice(h * HD, (h + 1) * HD)
            grad = jnp.concatenate(
                [ga[place(b) * TB : (place(b) + 1) * TB, cols] for b in range(SEQ // TB)], axis=0
            ).astype(BF)
            prob = probs[h]
            dprobs = nt(grad, v_ref[:, cols])
            center = jnp.sum(dprobs * prob, axis=-1, keepdims=True)
            grad_scores = (prob * (dprobs - center) * scale).astype(BF)
            dq_ref[:, cols] = nn(grad_scores, k_ref[:, cols]).astype(BF)
            dk_ref[:, cols] = tn(grad_scores, q_ref[:, cols]).astype(BF)
            dv_ref[:, cols] = tn(prob.astype(BF), grad).astype(BF)

    stage_code(0)
    stage_core(0)
    res_z.wait_recv()
    for k in steps:
        res_y[k, 1] = send(res_at(y, 1 - zh), res_at(y, 1 - zh), to_y(k))
    res_c = [send(res_ref, res_at(y, zh), to_c)]
    res_c.append(send(res_at(y, 1 - zh), res_at(y, 1 - zh), to_c))
    stage_code(1)
    stage_core(1)
    stage_y(0)
    stage_code(2)
    stage_z(0)
    stage_core(2)
    stage_y(1)
    stage_code(3)
    stage_z(1)
    stage_core(3)
    stage_y(2)
    stage_z(2)
    stage_y(3)
    stage_out(0)
    stage_out(1)
    attention_backward()
    stage_z(3)
    stage_out(2)
    outs = [stage_done(0), stage_done(1)]

    for k in steps:
        gx[k].wait_recv()
    for z_ in range(NZL):
        total = gp[x, z_].astype(F32)
        for k in range(3):
            total += gx_recv[k, z_].astype(F32)
        gx_sum[z_] = total.astype(BF)
    gz = {k: send(gx_sum.at[(zl + k) % NZL], gz_recv.at[k - 1], to_zl(k)) for k in steps}

    stage_out(3)
    outs += [stage_done(2), stage_done(3)]
    for k in steps:
        for zh_ in (0, 1):
            res_y[k, zh_].wait_recv()
            from_zh = zh if zh_ == 0 else 1 - zh
            at = res_at((y - k + NY) % NY, from_zh)
            res_c.append(send(at, at, to_c))

    for k in steps:
        gz[k].wait_recv()
    total = gx_sum[zl].astype(F32)
    for k in range(3):
        total += gz_recv[k].astype(F32)
    summed = total.astype(BF)
    for b in range(OWN):
        gw_ref[b * BLOCK : (b + 1) * BLOCK, :] = tn(
            enc[b], summed[b * CODE_W : (b + 1) * CODE_W]
        )

    for made in res_c:
        made.wait_recv()
    for copy in outs:
        copy.wait()
    own_res.wait()
    for made in sems.started:
        made.wait_send()


STEP_BLOCKS = 8


def close_kernel(
    resid_ref, cs_ref, dec_ref, dq_in, dk_in, dv_in, gw_in,
    out_ref, dq_ref, dk_ref, dv_ref, gw_ref, copy_sem,
):
    step = pl.program_id(0)
    copies = [
        pltpu.make_async_copy(src, dst, copy_sem.at[i])
        for i, (src, dst) in enumerate(
            ((dq_in, dq_ref), (dk_in, dk_ref), (dv_in, dv_ref), (gw_in, gw_ref))
        )
    ]

    @pl.when(step == 0)
    def _():
        for copy in copies:
            copy.start()

    depth, width = STEP_BLOCKS * CODE_W, STEP_BLOCKS * BLOCK
    row = lax.broadcasted_iota(jnp.int32, (depth, BLOCK), 0) // CODE_W
    dec = dec_ref[...]
    opened = jnp.concatenate(
        [jnp.where(row == b, dec, jnp.zeros_like(dec)) for b in range(STEP_BLOCKS)], axis=1
    )
    added = nn(cs_ref[0], opened)
    for b in range(SEQ // TB):
        p = place(b)
        out_ref[b * TB : (b + 1) * TB, :] = (
            resid_ref[b * TB : (b + 1) * TB, :].astype(F32) + added[p * TB : (p + 1) * TB]
        ).astype(BF)

    @pl.when(step == pl.num_programs(0) - 1)
    def _():
        for copy in copies:
            copy.wait()


def local(queries, key_rows, value_rows, residual_in, out_weight, encoder, decoder, grad_out):
    vmem = pl.BlockSpec(memory_space=pltpu.VMEM)
    anywhere = pl.BlockSpec(memory_space=pl.ANY)
    dec_rows = decoder.reshape(CODE, BLOCK)
    resid, code_sum, dq, dk, dv, gw = pl.pallas_call(
        main_kernel,
        out_shape=(
            jax.ShapeDtypeStruct((SEQ, D), BF),
            jax.ShapeDtypeStruct((NZL, SEQ, CH), BF),
            jax.ShapeDtypeStruct((SEQ, AW), BF),
            jax.ShapeDtypeStruct((SEQ, AW), BF),
            jax.ShapeDtypeStruct((SEQ, AW), BF),
            jax.ShapeDtypeStruct((OWN * BLOCK, AW), F32),
        ),
        in_specs=[vmem, vmem, vmem, anywhere, vmem, anywhere, vmem, vmem],
        out_specs=(anywhere, anywhere, vmem, vmem, vmem, vmem),
        scratch_shapes=[
            pltpu.VMEM((NZL, CH, AW), BF),
            pltpu.VMEM((NZL, SEQ, CH), BF),
            pltpu.VMEM((SEQ, AW), BF),
            pltpu.VMEM((HEADS, SEQ, SEQ), F32),
            pltpu.VMEM((SEQ, AW), F32),
            pltpu.VMEM((OWN, CODE_W, BLOCK), BF),
            pltpu.VMEM((4, HALF, CH), BF),
            pltpu.VMEM((4, HALF, CH), BF),
            pltpu.VMEM((4, HALF, CH), BF),
            pltpu.VMEM((4, HALF, CH), BF),
            pltpu.VMEM((4, 3, PAIR, CH), BF),
            pltpu.VMEM((4, PAIR, CH), BF),
            pltpu.VMEM((4, PAIR, CH), BF),
            pltpu.VMEM((NZL, SEQ, CH), BF),
            pltpu.VMEM((NX, NZL, ER, AW), BF),
            pltpu.VMEM((3, NZL, ER, AW), BF),
            pltpu.VMEM((NZL, ER, AW), BF),
            pltpu.VMEM((3, ER, AW), BF),
            pltpu.SemaphoreType.DMA((N_SEMS,)),
            pltpu.SemaphoreType.DMA((N_SEMS,)),
            pltpu.SemaphoreType.DMA((8,)),
        ],
        name="exchange",
        compiler_params=pltpu.CompilerParams(
            collective_id=0, has_side_effects=True, vmem_limit_bytes=48 * 2**20
        ),
    )(queries, key_rows, value_rows, residual_in, out_weight, encoder, dec_rows, grad_out)

    steps = NBLK // STEP_BLOCKS
    per = steps // NZL
    layer_out, dq, dk, dv, gw = pl.pallas_call(
        close_kernel,
        grid=(steps,),
        out_shape=(
            jax.ShapeDtypeStruct((SEQ, D), BF),
            jax.ShapeDtypeStruct((SEQ, AW), BF),
            jax.ShapeDtypeStruct((SEQ, AW), BF),
            jax.ShapeDtypeStruct((SEQ, AW), BF),
            jax.ShapeDtypeStruct((OWN * BLOCK, AW), F32),
        ),
        in_specs=[
            pl.BlockSpec((SEQ, STEP_BLOCKS * BLOCK), lambda i: (0, i)),
            pl.BlockSpec((1, SEQ, STEP_BLOCKS * CODE_W), lambda i: (i // per, 0, i % per)),
            pl.BlockSpec((STEP_BLOCKS * CODE_W, BLOCK), lambda i: (i, 0)),
            anywhere,
            anywhere,
            anywhere,
            anywhere,
        ],
        out_specs=(
            pl.BlockSpec((SEQ, STEP_BLOCKS * BLOCK), lambda i: (0, i)),
            anywhere,
            anywhere,
            anywhere,
            anywhere,
        ),
        scratch_shapes=[pltpu.SemaphoreType.DMA((4,))],
        name="close",
        compiler_params=pltpu.CompilerParams(vmem_limit_bytes=32 * 2**20),
    )(resid, code_sum, dec_rows, dq, dk, dv, gw)
    return layer_out, dq, dk, dv, gw


def solution(mesh):
    placed = (
        P("dp", "tensor"),
        P("dp", "tensor"),
        P("dp", "tensor"),
        P(("dp", "tensor"), None),
        P("dp", "tensor"),
        P(),
        P(),
        P(("dp", "tensor"), None),
    )
    return jax.shard_map(
        local,
        mesh=mesh,
        in_specs=placed,
        out_specs=(
            P("dp", None),
            P("dp", "tensor"),
            P("dp", "tensor"),
            P("dp", "tensor"),
            P("dp", "tensor"),
        ),
        check_vma=False,
    )
```

```python
import math

import jax
import jax.numpy as jnp
from jax import lax
from jax.experimental import pallas as pl
from jax.experimental.pallas import tpu as pltpu
from jax.sharding import PartitionSpec as P

HD = 128
NEG_FILL = -1e30
MESH = pl.DeviceIdType.MESH
BF, F32 = jnp.bfloat16, jnp.float32

NX, NZL, NY, NZH, NC = 4, 4, 4, 2, 2
TB = 16
SEQ = 256
HEADS = 3
AW = HEADS * HD
NBLK, CODE_W, BLOCK = 96, 32, 128
CODE = NBLK * CODE_W
D = NBLK * BLOCK
OWN = 6
ER = OWN * CODE_W
CH = NX * ER
HALF = SEQ // NC
PAIR = TB * NZH


def nt(a, b):
    return lax.dot_general(a, b, (((1,), (1,)), ((), ())), preferred_element_type=F32)


def nn(a, b):
    return lax.dot_general(a, b, (((1,), (0,)), ((), ())), preferred_element_type=F32)


def tn(a, b):
    return lax.dot_general(a, b, (((0,), (0,)), ((), ())), preferred_element_type=F32)


def place(t):
    return ((t % NC) * NY + t // (NC * NZH)) * NZH + (t // NC) % NZH


class Sems:
    def __init__(self, send, recv):
        self.send, self.recv, self.used, self.started = send, recv, 0, []

    def copy(self, src, dst, target):
        i = self.used
        self.used += 1
        made = pltpu.make_async_remote_copy(
            src_ref=src,
            dst_ref=dst,
            send_sem=self.send.at[i],
            recv_sem=self.recv.at[i],
            device_id=target,
            device_id_type=MESH,
        )
        made.start()
        self.started.append(made)
        return made


N_SEMS = 160
G_ORDER = (2, 1, 3, 0)
STEPS = (1, 3, 2)
PIECES = 2


def wait_for(ref, send_sem, recv_sem, target):
    pltpu.make_async_remote_copy(
        src_ref=ref,
        dst_ref=ref,
        send_sem=send_sem,
        recv_sem=recv_sem,
        device_id=target,
        device_id_type=MESH,
    ).wait_recv()


def main_kernel(
    q_hbm, k_hbm, v_hbm, res_ref, w_hbm, enc_hbm, dec_hbm, go_hbm,
    resid_ref, ag, dq_ref, dk_ref, dv_ref, gw_ref,
    q_ref, k_ref, v_ref, w_ref, enc, dec_ref, go_ref,
    ew, gcb, attn_p, probs, ga,
    c_own, c_send, c_recv, y_sum, y_recv, z_sum, z_recv,
    gp, g_via, g_mid, g_near, g_far, g_sum, gz_recv,
    send_sem, recv_sem, line_send, line_recv, local_sem,
):
    dp, t = lax.axis_index("dp"), lax.axis_index("tensor")
    zl, x = dp // NX, dp % NX
    y, zh, c = t // (NZH * NC), (t // NC) % NZH, t % NC

    def to_x(k):
        return (zl * NX + (x + k) % NX, t)

    def to_zl(k):
        return (((zl + k) % NZL) * NX + x, t)

    def to_y(k):
        return (dp, (((y + k) % NY) * NZH + zh) * NC + c)

    to_zh = (dp, (y * NZH + 1 - zh) * NC + c)
    to_c = (dp, (y * NZH + zh) * NC + 1 - c)

    sems = Sems(send_sem, recv_sem)
    send = sems.copy

    barrier = pltpu.get_barrier_semaphore()
    peers = [to_x(1), to_x(3)] + [to_zl(k) for k in STEPS]
    peers += [to_y(k) for k in STEPS] + [to_zh, to_c]
    for peer in peers:
        pl.semaphore_signal(barrier, inc=1, device_id=peer, device_id_type=MESH)

    own_rows = pl.ds(pl.multiple_of(t * TB, TB), TB)
    loads = {}
    for i, (name, src, dst) in enumerate((
        ("enc", enc_hbm.at[pl.ds(dp * OWN, OWN)], enc),
        ("w", w_hbm, w_ref),
        ("go", go_hbm, go_ref),
        ("dec", dec_hbm, dec_ref),
        ("q", q_hbm, q_ref),
        ("k", k_hbm, k_ref),
        ("v", v_hbm, v_ref),
        ("res", res_ref, resid_ref.at[own_rows]),
    )):
        loads[name] = pltpu.make_async_copy(src, dst, local_sem.at[i])
        loads[name].start()

    def ew_at(zl_, x_):
        return ew.at[zl_, pl.ds(pl.multiple_of(x_ * ER, ER), ER)]

    loads["enc"].wait()
    loads["w"].wait()
    for b in range(OWN):
        rows = pl.ds(pl.multiple_of(x * ER + b * CODE_W, CODE_W), CODE_W)
        ew[zl, rows, :] = nn(enc[b], w_ref[b * BLOCK : (b + 1) * BLOCK, :]).astype(BF)
    pl.semaphore_wait(barrier, len(peers))

    zls = [zl, zl + 1 - 2 * (zl % 2), 2 - zl // 2, 3 - 3 * (zl // 2)]

    def line_copy(slot, z_, step):
        return pltpu.make_async_remote_copy(
            src_ref=ew_at(z_, x),
            dst_ref=ew_at(z_, x),
            send_sem=line_send.at[slot],
            recv_sem=line_recv.at[z_],
            device_id=((zl + step) * NX + x, t),
            device_id_type=MESH,
        )

    line = [(zl < NZL - 1, 0, zl, 1), (zl > 0, 1, zl, -1)]
    for i in range(1, NZL):
        up = zls[i] < zl
        goes = jnp.logical_or(
            jnp.logical_and(up, zl < NZL - 1), jnp.logical_and(jnp.logical_not(up), zl > 0)
        )
        line.append((goes, 1 + i, zls[i], jnp.where(up, 1, -1)))

    def line_start(goes, *rest):
        @pl.when(goes)
        def _():
            line_copy(*rest).start()

    for entry in line[:2]:
        line_start(*entry)
    e_up, e_down, e_far = {}, {}, {}

    def weight_x(i):
        e_up[i] = send(ew_at(zls[i], x), ew_at(zls[i], x), to_x(1))
        e_down[i] = send(ew_at(zls[i], x), ew_at(zls[i], x), to_x(3))

    def weight_x2(i):
        if i % 2 == 0:
            e_up[i].wait_recv()
            at = ew_at(zls[i], (x + 3) % NX)
            e_far[i] = send(at, at, to_x(1))
        else:
            e_down[i].wait_recv()
            at = ew_at(zls[i], (x + 1) % NX)
            e_far[i] = send(at, at, to_x(3))

    weight_x(0)

    def place_of(y_, zh_, c_):
        return (c_ * NY + y_) * NZH + zh_

    def block_rows(p, n=1):
        return pl.ds(pl.multiple_of(p * TB, TB), TB * n)

    mine = block_rows(place_of(y, zh, c))
    other = block_rows(place_of(y, 1 - zh, c))
    lane_block = lax.broadcasted_iota(jnp.int32, (TB, BLOCK), 1) // CODE_W
    loads["res"].wait()
    loads["go"].wait()
    loads["dec"].wait()
    for g in range(NBLK // 4):
        wide = jnp.concatenate(
            [go_ref[:, (4 * g + j) * BLOCK : (4 * g + j + 1) * BLOCK] for j in range(4)], axis=0
        )
        coded = nt(wide, dec_ref[g * BLOCK : (g + 1) * BLOCK, :])
        picked = coded[:TB]
        for j in range(1, 4):
            picked = jnp.where(lane_block == j, coded[j * TB : (j + 1) * TB], picked)
        gcb[g // 6, mine, (g % 6) * BLOCK : (g % 6 + 1) * BLOCK] = picked.astype(BF)

    gc_y, gc_c = {}, []
    gc_z = send(gcb.at[:, mine], gcb.at[:, mine], to_zh)
    for k in STEPS:
        gc_y[k, 0] = send(gcb.at[:, mine], gcb.at[:, mine], to_y(k))

    def cotangent_y():
        gc_z.wait_recv()
        for k in STEPS:
            gc_y[k, 1] = send(gcb.at[:, other], gcb.at[:, other], to_y(k))
        pair = block_rows(place_of(y, 0, c), NZH)
        gc_c.append(send(gcb.at[:, pair], gcb.at[:, pair], to_c))

    def cotangent_c():
        for k in STEPS:
            gc_y[k, 0].wait_recv()
            gc_y[k, 1].wait_recv()
            pair = block_rows(place_of((y - k + NY) % NY, 0, c), NZH)
            gc_c.append(send(gcb.at[:, pair], gcb.at[:, pair], to_c))
        for made in gc_c:
            made.wait_recv()

    def res_at(y_, zh_, p):
        rows = pl.ds(pl.multiple_of((y_ * NZH + zh_) * (NC * TB) + c * TB, TB), TB)
        return resid_ref.at[rows, p * (D // PIECES) : (p + 1) * (D // PIECES)]

    res, res_c = {}, []
    shards = (zh, 1 - zh)

    def res_move(name, y_, i, p, target):
        at = res_at(y_, shards[i], p)
        res[name, i, p] = send(at, at, target)

    def res_core(y_, i, p):
        at = res_at(y_, shards[i], p)
        res_c.append(send(at, at, to_c))

    def res_z(p):
        res_move("z", y, 0, p, to_zh)

    def res_first(i, p):
        if i:
            res["z", 0, p].wait_recv()
        res_move("up", y, i, p, to_y(1))
        res_move("down", y, i, p, to_y(3))

    def res_second(i, p):
        res["up", i, p].wait_recv()
        if p % 2 == 0:
            res_move("far", (y + 3) % NY, i, p, to_y(1))
        res["down", i, p].wait_recv()
        if p % 2:
            res_move("far", (y + 1) % NY, i, p, to_y(3))

    def res_cores(i, p):
        res_core(y, i, p)
        res_core((y + 3) % NY, i, p)
        res_core((y + 1) % NY, i, p)

    def res_last(i, p):
        res["far", i, p].wait_recv()
        res_core((y + 2) % NY, i, p)

    scale = 1.0 / math.sqrt(HD)

    def attention_forward():
        for name in "qkv":
            loads[name].wait()
        row_index = lax.broadcasted_iota(jnp.int32, (SEQ, SEQ), 0)
        col_index = lax.broadcasted_iota(jnp.int32, (SEQ, SEQ), 1)
        for h in range(HEADS):
            cols = slice(h * HD, (h + 1) * HD)
            scores = nt(q_ref[:, cols], k_ref[:, cols]) * scale
            scores = jnp.where(col_index <= row_index, scores, NEG_FILL)
            weights = jnp.exp(scores - jnp.max(scores, axis=-1, keepdims=True))
            prob = weights / jnp.sum(weights, axis=-1, keepdims=True)
            probs[h] = prob
            mixed = nn(prob.astype(BF), v_ref[:, cols]).astype(BF)
            for b in range(SEQ // TB):
                p = place(b)
                attn_p[p * TB : (p + 1) * TB, cols] = mixed[b * TB : (b + 1) * TB]

    def attention_backward():
        for h in range(HEADS):
            cols = slice(h * HD, (h + 1) * HD)
            grad = jnp.concatenate(
                [ga[place(b) * TB : (place(b) + 1) * TB, cols] for b in range(SEQ // TB)], axis=0
            ).astype(BF)
            prob = probs[h]
            dprobs = nt(grad, v_ref[:, cols])
            center = jnp.sum(dprobs * prob, axis=-1, keepdims=True)
            grad_scores = (prob * (dprobs - center) * scale).astype(BF)
            dq_ref[:, cols] = nn(grad_scores, k_ref[:, cols]).astype(BF)
            dk_ref[:, cols] = tn(grad_scores, q_ref[:, cols]).astype(BF)
            dv_ref[:, cols] = tn(prob.astype(BF), grad).astype(BF)

    g_up, g_down, g_on, gz = {}, {}, {}, {}

    def grad_start(i):
        z_ = (zl + G_ORDER[i]) % NZL
        term = tn(gcb[z_], attn_p[...])
        for x_ in range(NX):
            gp[i, x_] = term[x_ * ER : (x_ + 1) * ER].astype(BF)
        far = gp.at[i, (x + 2) % NX]
        if i % 2 == 0:
            g_up[i] = send(far, g_via.at[i], to_x(1))
            g_down[i] = send(gp.at[i, (x + 3) % NX], g_near.at[i], to_x(3))
        else:
            g_down[i] = send(far, g_via.at[i], to_x(3))
            g_up[i] = send(gp.at[i, (x + 1) % NX], g_near.at[i], to_x(1))

    def grad_on(i):
        step = 1 if i % 2 == 0 else 3
        (g_up if i % 2 == 0 else g_down)[i].wait_recv()
        g_mid[i] = (gp[i, (x + step) % NX].astype(F32) + g_via[i].astype(F32)).astype(BF)
        g_on[i] = send(g_mid.at[i], g_far.at[i], to_x(step))

    def grad_z(i):
        (g_down if i % 2 == 0 else g_up)[i].wait_recv()
        g_on[i].wait_recv()
        total = gp[i, x].astype(F32) + g_near[i].astype(F32) + g_far[i].astype(F32)
        g_sum[i] = total.astype(BF)
        k = G_ORDER[i]
        if k:
            gz[k] = send(g_sum.at[i], gz_recv.at[k - 1], to_zl(k))

    def grad_end():
        total = g_sum[G_ORDER.index(0)].astype(F32)
        for k in STEPS:
            gz[k].wait_recv()
            total += gz_recv[k - 1].astype(F32)
        summed = total.astype(BF)
        for b in range(OWN):
            gw_ref[b * BLOCK : (b + 1) * BLOCK, :] = tn(
                enc[b], summed[b * CODE_W : (b + 1) * CODE_W]
            )

    c_cp, y_cp, z_cp, a_cp, ac_cp = {}, {}, {}, {}, {}

    def code(i):
        (e_down if i % 2 == 0 else e_up)[i].wait_recv()
        e_far[i].wait_recv()
        codes = nt(attn_p[...], ew[zls[i]]).astype(BF)
        for half in range(NC):
            part = codes[half * HALF : (half + 1) * HALF]

            @pl.when(c == half)
            def _():
                c_own[i] = part

            @pl.when(c != half)
            def _():
                c_send[i] = part

        c_cp[i] = send(c_send.at[i], c_recv.at[i], to_c)

    def grad_attn(i):
        grown = nn(gcb[zls[i]], ew[zls[i]])
        if i == 0:
            ga[...] = grown
        else:
            ga[...] += grown

    def code_y(i):
        c_cp[i].wait_recv()
        y_sum[i] = (c_own[i].astype(F32) + c_recv[i].astype(F32)).astype(BF)
        for k in STEPS:
            rows = pl.ds(pl.multiple_of(((y + k) % NY) * PAIR, PAIR), PAIR)
            y_cp[i, k] = send(y_sum.at[i, rows], y_recv.at[i, k - 1], to_y(k))

    def code_z(i):
        for k in STEPS:
            y_cp[i, k].wait_recv()
        rows = pl.ds(pl.multiple_of(y * PAIR, PAIR), PAIR)
        total = y_sum[i, rows].astype(F32)
        for k in range(3):
            total += y_recv[i, k].astype(F32)
        z_sum[i] = total.astype(BF)
        z_cp[i] = send(z_sum.at[i], z_recv.at[i], to_zh)

    def ag_at(z_, y_):
        return ag.at[z_, pl.ds(pl.multiple_of((c * NY + y_) * PAIR, PAIR), PAIR)]

    def code_back(i):
        z_cp[i].wait_recv()
        at = ag_at(zls[i], y)
        at[...] = (z_sum[i].astype(F32) + z_recv[i].astype(F32)).astype(BF)
        for k in STEPS:
            a_cp[i, k] = send(at, at, to_y(k))
        ac_cp[i, 0] = send(at, at, to_c)

    def code_out(i):
        for k in STEPS:
            a_cp[i, k].wait_recv()
            at = ag_at(zls[i], (y - k + NY) % NY)
            ac_cp[i, k] = send(at, at, to_c)

    def code_done(i):
        for k in (0,) + STEPS:
            ac_cp[i, k].wait_recv()

    def weight_z(i):
        at = ew_at(zls[i], x)
        wait_for(at, line_send.at[0], line_recv.at[zls[i]], to_zl(1))
        line_start(*line[1 + i])
        weight_x(i)

    res_first(0, 0)
    attention_forward()
    weight_x2(0)
    weight_z(1)
    weight_z(2)
    code(0)
    weight_x2(1)
    cotangent_y()
    weight_z(3)
    res_z(0)
    res_first(0, 1)
    code_y(0)
    res_second(0, 0)
    res_cores(0, 0)
    weight_x2(2)
    code(1)
    cotangent_c()
    res_z(1)
    grad_start(0)
    code_y(1)
    code_z(0)
    weight_x2(3)
    code(2)
    code_y(2)
    grad_attn(0)
    grad_attn(1)
    grad_attn(2)
    code(3)
    grad_start(1)
    code_y(3)
    grad_on(0)
    grad_start(2)
    grad_start(3)
    code_z(1)
    res_second(0, 1)
    res_cores(0, 1)
    code_z(2)
    res_first(1, 0)
    code_back(0)
    grad_on(1)
    grad_attn(3)
    attention_backward()
    code_z(3)
    grad_z(0)
    grad_on(2)
    code_back(1)
    code_out(0)
    res_first(1, 1)
    grad_z(1)
    grad_on(3)
    code_back(2)
    res_second(1, 0)
    res_cores(1, 0)
    code_out(1)
    grad_z(2)
    grad_z(3)
    code_back(3)
    res_last(0, 0)
    res_last(0, 1)
    code_out(2)
    res_second(1, 1)
    res_cores(1, 1)
    code_out(3)
    for i in range(NZL):
        code_done(i)
    grad_end()
    res_last(1, 0)
    res_last(1, 1)

    for made in res_c:
        made.wait_recv()
    for goes, *rest in line:

        @pl.when(goes)
        def _():
            line_copy(*rest).wait_send()

    for made in sems.started:
        made.wait_send()


STEP_BLOCKS = 8
CLOSE_STEPS = NBLK // STEP_BLOCKS


def close_kernel(
    resid_ref, cs_ref, dec_hbm, dq_in, dk_in, dv_in, gw_in,
    out_ref, dq_ref, dk_ref, dv_ref, gw_ref, dec_ref, layer, copy_sem, out_sem,
):
    load = pltpu.make_async_copy(dec_hbm, dec_ref, copy_sem.at[4])
    load.start()
    copies = [
        pltpu.make_async_copy(src, dst, copy_sem.at[i])
        for i, (src, dst) in enumerate(
            ((dq_in, dq_ref), (dk_in, dk_ref), (dv_in, dv_ref), (gw_in, gw_ref))
        )
    ]
    for copy in copies:
        copy.start()
    load.wait()
    depth, width = STEP_BLOCKS * CODE_W, STEP_BLOCKS * BLOCK
    per = CLOSE_STEPS // NZL
    row = lax.broadcasted_iota(jnp.int32, (depth, BLOCK), 0) // CODE_W
    for step in range(CLOSE_STEPS):
        cols = slice(step * width, (step + 1) * width)
        dec = dec_ref[step * depth : (step + 1) * depth, :]
        opened = jnp.concatenate(
            [jnp.where(row == b, dec, jnp.zeros_like(dec)) for b in range(STEP_BLOCKS)], axis=1
        )
        codes = cs_ref[step // per, :, (step % per) * depth : (step % per + 1) * depth]
        added = nn(codes, opened)
        for b in range(SEQ // TB):
            p = place(b)
            rows = slice(b * TB, (b + 1) * TB)
            layer[rows, cols] = (
                resid_ref[rows, cols].astype(F32) + added[p * TB : (p + 1) * TB]
            ).astype(BF)
        copies.append(
            pltpu.make_async_copy(layer.at[:, cols], out_ref.at[:, cols], out_sem.at[step])
        )
        copies[-1].start()
    for copy in copies:
        copy.wait()


def local(queries, key_rows, value_rows, residual_in, out_weight, encoder, decoder, grad_out):
    vmem = pl.BlockSpec(memory_space=pltpu.VMEM)
    anywhere = pl.BlockSpec(memory_space=pl.ANY)
    dec_rows = decoder.reshape(CODE, BLOCK)
    operands = (queries, key_rows, value_rows, residual_in, out_weight, encoder, dec_rows, grad_out)
    operands = [pltpu.with_memory_space_constraint(a, pltpu.HBM) for a in operands]
    dec_rows = operands[6]
    resid, code_sum, dq, dk, dv, gw = pl.pallas_call(
        main_kernel,
        out_shape=(
            pltpu.VMEM((SEQ, D), BF),
            pltpu.VMEM((NZL, SEQ, CH), BF),
            pltpu.VMEM((SEQ, AW), BF),
            pltpu.VMEM((SEQ, AW), BF),
            pltpu.VMEM((SEQ, AW), BF),
            pltpu.VMEM((OWN * BLOCK, AW), F32),
        ),
        in_specs=[anywhere] * 8,
        out_specs=(vmem,) * 6,
        scratch_shapes=[
            pltpu.VMEM((SEQ, AW), BF),
            pltpu.VMEM((SEQ, AW), BF),
            pltpu.VMEM((SEQ, AW), BF),
            pltpu.VMEM((OWN * BLOCK, AW), BF),
            pltpu.VMEM((OWN, CODE_W, BLOCK), BF),
            pltpu.VMEM((CODE, BLOCK), BF),
            pltpu.VMEM((TB, D), BF),
            pltpu.VMEM((NZL, CH, AW), BF),
            pltpu.VMEM((NZL, SEQ, CH), BF),
            pltpu.VMEM((SEQ, AW), BF),
            pltpu.VMEM((HEADS, SEQ, SEQ), F32),
            pltpu.VMEM((SEQ, AW), F32),
            pltpu.VMEM((4, HALF, CH), BF),
            pltpu.VMEM((4, HALF, CH), BF),
            pltpu.VMEM((4, HALF, CH), BF),
            pltpu.VMEM((4, HALF, CH), BF),
            pltpu.VMEM((4, 3, PAIR, CH), BF),
            pltpu.VMEM((4, PAIR, CH), BF),
            pltpu.VMEM((4, PAIR, CH), BF),
            pltpu.VMEM((NZL, NX, ER, AW), BF),
            pltpu.VMEM((NZL, ER, AW), BF),
            pltpu.VMEM((NZL, ER, AW), BF),
            pltpu.VMEM((NZL, ER, AW), BF),
            pltpu.VMEM((NZL, ER, AW), BF),
            pltpu.VMEM((NZL, ER, AW), BF),
            pltpu.VMEM((3, ER, AW), BF),
            pltpu.SemaphoreType.DMA((N_SEMS,)),
            pltpu.SemaphoreType.DMA((N_SEMS,)),
            pltpu.SemaphoreType.DMA((5,)),
            pltpu.SemaphoreType.DMA((NZL,)),
            pltpu.SemaphoreType.DMA((8,)),
        ],
        name="exchange",
        compiler_params=pltpu.CompilerParams(
            collective_id=0, has_side_effects=True, vmem_limit_bytes=32 * 2**20
        ),
    )(*operands)

    return pl.pallas_call(
        close_kernel,
        out_shape=(
            pltpu.HBM((SEQ, D), BF),
            pltpu.HBM((SEQ, AW), BF),
            pltpu.HBM((SEQ, AW), BF),
            pltpu.HBM((SEQ, AW), BF),
            pltpu.HBM((OWN * BLOCK, AW), F32),
        ),
        in_specs=[vmem, vmem, anywhere, vmem, vmem, vmem, vmem],
        out_specs=(anywhere,) * 5,
        scratch_shapes=[
            pltpu.VMEM((CODE, BLOCK), BF),
            pltpu.VMEM((SEQ, D), BF),
            pltpu.SemaphoreType.DMA((5,)),
            pltpu.SemaphoreType.DMA((CLOSE_STEPS,)),
        ],
        name="close",
        compiler_params=pltpu.CompilerParams(vmem_limit_bytes=20 * 2**20),
    )(resid, code_sum, dec_rows, dq, dk, dv, gw)


def solution(mesh):
    placed = (
        P("dp", "tensor"),
        P("dp", "tensor"),
        P("dp", "tensor"),
        P(("dp", "tensor"), None),
        P("dp", "tensor"),
        P(),
        P(),
        P(("dp", "tensor"), None),
    )
    return jax.shard_map(
        local,
        mesh=mesh,
        in_specs=placed,
        out_specs=(
            P("dp", None),
            P("dp", "tensor"),
            P("dp", "tensor"),
            P("dp", "tensor"),
            P("dp", "tensor"),
        ),
        check_vma=False,
    )
```

```python
import math

import jax
import jax.numpy as jnp
from jax import lax
from jax.experimental import pallas as pl
from jax.experimental.pallas import tpu as pltpu
from jax.sharding import PartitionSpec as P

HD = 128
NEG_FILL = -1e30
MESH = pl.DeviceIdType.MESH
BF, F32 = jnp.bfloat16, jnp.float32

NX, NZL, NY, NZH, NC = 4, 4, 4, 2, 2
TB = 16
SEQ = 256
HEADS = 3
AW = HEADS * HD
NBLK, CODE_W, BLOCK = 96, 32, 128
CODE = NBLK * CODE_W
D = NBLK * BLOCK
OWN = 6
ER = OWN * CODE_W
CH = NX * ER
HALF = SEQ // NC
PAIR = TB * NZH


def nt(a, b):
    return lax.dot_general(a, b, (((1,), (1,)), ((), ())), preferred_element_type=F32)


def nn(a, b):
    return lax.dot_general(a, b, (((1,), (0,)), ((), ())), preferred_element_type=F32)


def tn(a, b):
    return lax.dot_general(a, b, (((0,), (0,)), ((), ())), preferred_element_type=F32)


def place(t):
    return ((t % NC) * NY + t // (NC * NZH)) * NZH + (t // NC) % NZH


N_SEND, N_RECV = 48, 96


class Sems:
    def __init__(self, send, recv):
        self.send, self.recv, self.groups, self.used, self.started = send, recv, {}, 0, []

    def slot(self, group):
        if group not in self.groups:
            self.groups[group] = self.used
            self.used += 1
        return self.recv.at[self.groups[group]]

    def copy(self, src, dst, target, group=None):
        n = len(self.started)
        if n >= N_SEND:
            self.started[n - N_SEND].wait_send()
        made = pltpu.make_async_remote_copy(
            src_ref=src,
            dst_ref=dst,
            send_sem=self.send.at[n % N_SEND],
            recv_sem=self.slot(n if group is None else group),
            device_id=target,
            device_id_type=MESH,
        )
        made.start()
        self.started.append(made)
        return made

    def arrived(self, ref, group, target):
        wait_for(ref, self.send.at[0], self.slot(group), target)

G_ORDER = (1, 3, 2, 0)
STEPS = (1, 3, 2)
PIECES = 4


def wait_for(ref, send_sem, recv_sem, target):
    pltpu.make_async_remote_copy(
        src_ref=ref,
        dst_ref=ref,
        send_sem=send_sem,
        recv_sem=recv_sem,
        device_id=target,
        device_id_type=MESH,
    ).wait_recv()


def main_kernel(
    q_hbm, k_hbm, v_hbm, res_ref, w_hbm, enc_hbm, dec_hbm, go_hbm,
    resid_ref, ag, dq_ref, dk_ref, dv_ref, gw_ref, dec_ref,
    q_ref, k_ref, v_ref, w_ref, enc, go_ref,
    ew, gcb, attn_p, probs, ga,
    c_own, c_send, c_recv, y_sum, y_via, y_mid, y_near, y_far, z_sum, z_recv,
    gp, g_via, g_mid, g_near, g_far, g_sum, gz_recv, gz_via,
    send_sem, recv_sem, line_send, line_recv, gz_send, gz_arrive, local_sem,
):
    dp, t = lax.axis_index("dp"), lax.axis_index("tensor")
    zl, x = dp // NX, dp % NX
    y, zh, c = t // (NZH * NC), (t // NC) % NZH, t % NC

    def to_x(k):
        return (zl * NX + (x + k) % NX, t)

    def to_zl(k):
        return (((zl + k) % NZL) * NX + x, t)

    def to_y(k):
        return (dp, (((y + k) % NY) * NZH + zh) * NC + c)

    to_zh = (dp, (y * NZH + 1 - zh) * NC + c)
    to_c = (dp, (y * NZH + zh) * NC + 1 - c)

    sems = Sems(send_sem, recv_sem)
    send = sems.copy

    barrier = pltpu.get_barrier_semaphore()
    peers = [to_x(1), to_x(3)] + [to_zl(k) for k in STEPS]
    peers += [to_y(1), to_y(3), to_zh, to_c]
    for peer in peers:
        pl.semaphore_signal(barrier, inc=1, device_id=peer, device_id_type=MESH)

    own_rows = pl.ds(pl.multiple_of(t * TB, TB), TB)
    loads = {}
    for i, (name, src, dst) in enumerate((
        ("enc", enc_hbm.at[pl.ds(dp * OWN, OWN)], enc),
        ("w", w_hbm, w_ref),
        ("go", go_hbm, go_ref),
        ("dec", dec_hbm, dec_ref),
        ("q", q_hbm, q_ref),
        ("k", k_hbm, k_ref),
        ("v", v_hbm, v_ref),
        ("res", res_ref, resid_ref.at[own_rows]),
    )):
        loads[name] = pltpu.make_async_copy(src, dst, local_sem.at[i])
        loads[name].start()

    def ew_at(zl_, x_):
        return ew.at[zl_, pl.ds(pl.multiple_of(x_ * ER, ER), ER)]

    loads["enc"].wait()
    loads["w"].wait()
    for b in range(OWN):
        rows = pl.ds(pl.multiple_of(x * ER + b * CODE_W, CODE_W), CODE_W)
        ew[zl, rows, :] = nn(enc[b], w_ref[b * BLOCK : (b + 1) * BLOCK, :]).astype(BF)
    pl.semaphore_wait(barrier, len(peers))

    zls = [zl, zl + 1 - 2 * (zl % 2), 2 - zl // 2, 3 - 3 * (zl // 2)]

    def line_copy(slot, z_, step):
        return pltpu.make_async_remote_copy(
            src_ref=ew_at(z_, x),
            dst_ref=ew_at(z_, x),
            send_sem=line_send.at[slot],
            recv_sem=line_recv.at[z_],
            device_id=((zl + step) * NX + x, t),
            device_id_type=MESH,
        )

    line = [(zl < NZL - 1, 0, zl, 1), (zl > 0, 1, zl, -1)]
    for i in range(1, NZL):
        up = zls[i] < zl
        goes = jnp.logical_or(
            jnp.logical_and(up, zl < NZL - 1), jnp.logical_and(jnp.logical_not(up), zl > 0)
        )
        line.append((goes, 1 + i, zls[i], jnp.where(up, 1, -1)))

    def line_start(goes, *rest):
        @pl.when(goes)
        def _():
            line_copy(*rest).start()

    for entry in line[:2]:
        line_start(*entry)
    e_up, e_down, e_far = {}, {}, {}

    def weight_x(i):
        e_up[i] = send(ew_at(zls[i], x), ew_at(zls[i], x), to_x(1))
        e_down[i] = send(ew_at(zls[i], x), ew_at(zls[i], x), to_x(3))

    def weight_x2(i):
        if i % 2 == 0:
            e_up[i].wait_recv()
            at = ew_at(zls[i], (x + 3) % NX)
            e_far[i] = send(at, at, to_x(1))
        else:
            e_down[i].wait_recv()
            at = ew_at(zls[i], (x + 1) % NX)
            e_far[i] = send(at, at, to_x(3))

    weight_x(0)

    def place_of(y_, zh_, c_):
        return (c_ * NY + y_) * NZH + zh_

    def block_rows(p, n=1):
        return pl.ds(pl.multiple_of(p * TB, TB), TB * n)

    mine = block_rows(place_of(y, zh, c))
    other = block_rows(place_of(y, 1 - zh, c))
    lane_block = lax.broadcasted_iota(jnp.int32, (TB, BLOCK), 1) // CODE_W
    loads["res"].wait()
    loads["go"].wait()
    loads["dec"].wait()
    for g in range(NBLK // 4):
        wide = jnp.concatenate(
            [go_ref[:, (4 * g + j) * BLOCK : (4 * g + j + 1) * BLOCK] for j in range(4)], axis=0
        )
        coded = nt(wide, dec_ref[g * BLOCK : (g + 1) * BLOCK, :])
        picked = coded[:TB]
        for j in range(1, 4):
            picked = jnp.where(lane_block == j, coded[j * TB : (j + 1) * TB], picked)
        gcb[g // 6, mine, (g % 6) * BLOCK : (g % 6 + 1) * BLOCK] = picked.astype(BF)

    gc_up, gc_down, gc_far = {}, {}, {}
    gc_z = send(gcb.at[:, mine], gcb.at[:, mine], to_zh)

    def cotangent_first(i):
        at = gcb.at[:, (mine, other)[i]]
        gc_up[i] = send(at, at, to_y(1))
        gc_down[i] = send(at, at, to_y(3))

    def cotangent_core(y_):
        at = gcb.at[:, block_rows(place_of(y_, 0, c), NZH)]
        send(at, at, to_c, "gc")

    def cotangent_y():
        gc_z.wait_recv()
        cotangent_first(1)
        cotangent_core(y)

    def cotangent_relay():
        gc_up[0].wait_recv()
        at = gcb.at[:, block_rows(place_of((y + 3) % NY, zh, c))]
        gc_far[0] = send(at, at, to_y(1))
        gc_down[0].wait_recv()
        gc_down[1].wait_recv()
        at = gcb.at[:, block_rows(place_of((y + 1) % NY, 1 - zh, c))]
        gc_far[1] = send(at, at, to_y(3))
        cotangent_core((y + 1) % NY)
        gc_up[1].wait_recv()
        cotangent_core((y + 3) % NY)

    def cotangent_c():
        gc_far[0].wait_recv()
        gc_far[1].wait_recv()
        cotangent_core((y + 2) % NY)
        sems.arrived(gcb.at[:, :HALF], "gc", to_c)

    cotangent_first(0)

    def res_at(y_, zh_, p):
        rows = pl.ds(pl.multiple_of((y_ * NZH + zh_) * (NC * TB) + c * TB, TB), TB)
        return resid_ref.at[rows, p * (D // PIECES) : (p + 1) * (D // PIECES)]

    res = {}
    shards = (zh, 1 - zh)

    def res_move(name, y_, i, p, target):
        at = res_at(y_, shards[i], p)
        res[name, i, p] = send(at, at, target)

    def res_core(y_, i, half):
        rows = pl.ds(pl.multiple_of((y_ * NZH + shards[i]) * (NC * TB) + c * TB, TB), TB)
        at = resid_ref.at[rows, half * (D // 2) : (half + 1) * (D // 2)]
        send(at, at, to_c, "res")

    def res_z(p):
        res_move("z", y, 0, p, to_zh)

    def res_first(i, p):
        if i:
            res["z", 0, p].wait_recv()
        res_move("up", y, i, p, to_y(1))
        res_move("down", y, i, p, to_y(3))

    def res_second(i, p):
        res["up", i, p].wait_recv()
        if p % 2 == 0:
            res_move("far", (y + 3) % NY, i, p, to_y(1))
        res["down", i, p].wait_recv()
        if p % 2:
            res_move("far", (y + 1) % NY, i, p, to_y(3))

    def res_cores(i, half):
        res_core(y, i, half)
        res_core((y + 3) % NY, i, half)
        res_core((y + 1) % NY, i, half)

    def res_last(i, half):
        for p in (2 * half, 2 * half + 1):
            res["far", i, p].wait_recv()
        res_core((y + 2) % NY, i, half)

    scale = 1.0 / math.sqrt(HD)

    def attention_forward():
        grad_slot(1, True)
        grad_slot(3, True)
        for name in "qkv":
            loads[name].wait()
        row_index = lax.broadcasted_iota(jnp.int32, (SEQ, SEQ), 0)
        col_index = lax.broadcasted_iota(jnp.int32, (SEQ, SEQ), 1)
        for h in range(HEADS):
            cols = slice(h * HD, (h + 1) * HD)
            scores = nt(q_ref[:, cols], k_ref[:, cols]) * scale
            scores = jnp.where(col_index <= row_index, scores, NEG_FILL)
            weights = jnp.exp(scores - jnp.max(scores, axis=-1, keepdims=True))
            prob = weights / jnp.sum(weights, axis=-1, keepdims=True)
            probs[h] = prob
            mixed = nn(prob.astype(BF), v_ref[:, cols]).astype(BF)
            for b in range(SEQ // TB):
                p = place(b)
                attn_p[p * TB : (p + 1) * TB, cols] = mixed[b * TB : (b + 1) * TB]

    def attention_backward():
        for h in range(HEADS):
            cols = slice(h * HD, (h + 1) * HD)
            grad = jnp.concatenate(
                [ga[place(b) * TB : (place(b) + 1) * TB, cols] for b in range(SEQ // TB)], axis=0
            ).astype(BF)
            prob = probs[h]
            dprobs = nt(grad, v_ref[:, cols])
            center = jnp.sum(dprobs * prob, axis=-1, keepdims=True)
            grad_scores = (prob * (dprobs - center) * scale).astype(BF)
            dq_ref[:, cols] = nn(grad_scores, k_ref[:, cols]).astype(BF)
            dk_ref[:, cols] = tn(grad_scores, q_ref[:, cols]).astype(BF)
            dv_ref[:, cols] = tn(prob.astype(BF), grad).astype(BF)

    g_up, g_down, g_on = {}, {}, {}

    def grad_start(i):
        z_ = (zl + G_ORDER[i]) % NZL
        term = tn(gcb[z_], attn_p[...])
        for x_ in range(NX):
            gp[i, x_] = term[x_ * ER : (x_ + 1) * ER].astype(BF)
        far = gp.at[i, (x + 2) % NX]
        if i % 2 == 0:
            g_up[i] = send(far, g_via.at[i], to_x(1))
            g_down[i] = send(gp.at[i, (x + 3) % NX], g_near.at[i], to_x(3))
        else:
            g_down[i] = send(far, g_via.at[i], to_x(3))
            g_up[i] = send(gp.at[i, (x + 1) % NX], g_near.at[i], to_x(1))

    def grad_on(i):
        step = 1 if i % 2 == 0 else 3
        (g_up if i % 2 == 0 else g_down)[i].wait_recv()
        g_mid[i] = (gp[i, (x + step) % NX].astype(F32) + g_via[i].astype(F32)).astype(BF)
        g_on[i] = send(g_mid.at[i], g_far.at[i], to_x(step))

    def grad_z(i):
        (g_down if i % 2 == 0 else g_up)[i].wait_recv()
        g_on[i].wait_recv()
        total = gp[i, x].astype(F32) + g_near[i].astype(F32) + g_far[i].astype(F32)
        g_sum[i] = total.astype(BF)
        k = G_ORDER[i]
        if k == 2:
            @pl.when(inner)
            def _():
                wait_for(gz_via, gz_send.at[0], gz_arrive.at[3], to_zl(1))
                g_sum[i] = (total + gz_via[...].astype(F32)).astype(BF)

        if k:
            ends = zl == (-1, NZL - 1, -1, 0)[k]
            step = {1: -1, 3: 1, 2: 0}[k]

            @pl.when(jnp.logical_not(ends))
            def _():
                grad_copy(i, gz_recv.at[k - 1], k - 1, to_zl(k)).start()

            @pl.when(ends)
            def _():
                grad_copy(i, gz_via, 3, ((zl + step) * NX + x, t)).start()

    inner = jnp.logical_and(zl > 0, zl < NZL - 1)

    def grad_copy(i, dst, slot, target):
        return pltpu.make_async_remote_copy(
            src_ref=g_sum.at[i],
            dst_ref=dst,
            send_sem=gz_send.at[i],
            recv_sem=gz_arrive.at[slot],
            device_id=target,
            device_id_type=MESH,
        )

    def grad_slot(k, first):
        lone = zl == {1: 0, 2: -1, 3: NZL - 1}[k]

        @pl.when(lone if first else jnp.logical_not(lone))
        def _():
            if first:
                gz_recv[k - 1] = jnp.zeros((ER, AW), BF)
            else:
                wait_for(gz_recv.at[k - 1], gz_send.at[0], gz_arrive.at[k - 1], to_zl(1))

    def grad_end():
        total = g_sum[G_ORDER.index(0)].astype(F32)
        for k in STEPS:
            grad_slot(k, False)
            total += gz_recv[k - 1].astype(F32)
        summed = total.astype(BF)
        for b in range(OWN):
            gw_ref[b * BLOCK : (b + 1) * BLOCK, :] = tn(
                enc[b], summed[b * CODE_W : (b + 1) * CODE_W]
            )

    c_cp, y_cp, z_cp, a_cp = {}, {}, {}, {}

    def code(i):
        (e_down if i % 2 == 0 else e_up)[i].wait_recv()
        e_far[i].wait_recv()
        codes = nt(attn_p[...], ew[zls[i]]).astype(BF)
        for half in range(NC):
            part = codes[half * HALF : (half + 1) * HALF]

            @pl.when(c == half)
            def _():
                c_own[i] = part

            @pl.when(c != half)
            def _():
                c_send[i] = part

        c_cp[i] = send(c_send.at[i], c_recv.at[i], to_c)

    def grad_attn(i):
        grown = nn(gcb[zls[i]], ew[zls[i]])
        if i == 0:
            ga[...] = grown
        else:
            ga[...] += grown

    def y_block(i, k):
        return y_sum.at[i, pl.ds(pl.multiple_of(((y + k) % NY) * PAIR, PAIR), PAIR)]

    def code_y(i):
        c_cp[i].wait_recv()
        y_sum[i] = (c_own[i].astype(F32) + c_recv[i].astype(F32)).astype(BF)
        step = 1 if i % 2 == 0 else 3
        y_cp[i, "via"] = send(y_block(i, 2), y_via.at[i], to_y(step))
        y_cp[i, "near"] = send(y_block(i, 4 - step), y_near.at[i], to_y(4 - step))

    def code_mid(i):
        step = 1 if i % 2 == 0 else 3
        y_cp[i, "via"].wait_recv()
        y_mid[i] = (y_block(i, step)[...].astype(F32) + y_via[i].astype(F32)).astype(BF)
        y_cp[i, "far"] = send(y_mid.at[i], y_far.at[i], to_y(step))

    def code_z(i):
        y_cp[i, "near"].wait_recv()
        y_cp[i, "far"].wait_recv()
        total = y_block(i, 0)[...].astype(F32) + y_near[i].astype(F32) + y_far[i].astype(F32)
        z_sum[i] = total.astype(BF)
        z_cp[i] = send(z_sum.at[i], z_recv.at[i], to_zh)

    def ag_at(z_, y_):
        return ag.at[z_, pl.ds(pl.multiple_of((c * NY + y_) * PAIR, PAIR), PAIR)]

    def code_back(i):
        z_cp[i].wait_recv()
        at = ag_at(zls[i], y)
        at[...] = (z_sum[i].astype(F32) + z_recv[i].astype(F32)).astype(BF)
        a_cp[i, "up"] = send(at, at, to_y(1))
        a_cp[i, "down"] = send(at, at, to_y(3))
        send(at, at, to_c, "ag")

    def code_out(i):
        for name, k in (("up", 3), ("down", 1)):
            a_cp[i, name].wait_recv()
            at = ag_at(zls[i], (y + k) % NY)
            if name == ("up", "down")[i % 2]:
                a_cp[i, "far"] = send(at, at, to_y(4 - k))
            send(at, at, to_c, "ag")

    def code_far(i):
        a_cp[i, "far"].wait_recv()
        at = ag_at(zls[i], (y + 2) % NY)
        send(at, at, to_c, "ag")

    def code_done():
        sems.arrived(ag.at[:, :HALF], "ag", to_c)

    def res_done():
        sems.arrived(resid_ref.at[:HALF], "res", to_c)

    def sends_done():
        for goes, *rest in line:

            @pl.when(goes)
            def _():
                line_copy(*rest).wait_send()

        for i in range(NZL):
            if G_ORDER[i]:
                grad_copy(i, gz_recv.at[0], 0, to_zl(1)).wait_send()
        for made in sems.started[-N_SEND:]:
            made.wait_send()

    def weight_z(i):
        at = ew_at(zls[i], x)
        wait_for(at, line_send.at[0], line_recv.at[zls[i]], to_zl(1))
        line_start(*line[1 + i])
        weight_x(i)

    for p in range(PIECES):
        res_first(0, p)
    attention_forward()
    weight_x2(0)
    weight_z(1)
    weight_z(2)
    code(0)
    weight_x2(1)
    cotangent_y()
    weight_z(3)
    res_z(0)
    code_y(0)
    weight_x2(2)
    res_z(1)
    cotangent_relay()
    res_second(0, 0)
    res_second(0, 1)
    res_cores(0, 0)
    code_mid(0)
    code(1)
    code_y(1)
    weight_x2(3)
    res_second(0, 2)
    res_z(2)
    code(2)
    cotangent_c()
    grad_start(0)
    grad_start(1)
    code_mid(1)
    code_y(2)
    res_first(1, 0)
    code_z(0)
    res_z(3)
    code(3)
    code_y(3)
    res_second(0, 3)
    res_cores(0, 1)
    grad_start(2)
    code_z(1)
    code_mid(2)
    res_first(1, 1)
    grad_on(0)
    grad_start(3)
    grad_attn(0)
    grad_attn(1)
    grad_attn(2)
    grad_attn(3)
    code_mid(3)
    grad_on(1)
    code_back(0)
    code_z(2)
    attention_backward()
    grad_on(2)
    code_z(3)
    res_first(1, 2)
    grad_z(0)
    grad_on(3)
    code_back(1)
    code_out(0)
    grad_z(1)
    res_second(1, 0)
    res_second(1, 1)
    res_first(1, 3)
    code_back(2)
    grad_z(3)
    code_out(1)
    code_back(3)
    res_cores(1, 0)
    res_second(1, 2)
    grad_z(2)
    code_out(2)
    code_far(0)
    code_far(1)
    res_last(0, 0)
    res_last(0, 1)
    code_out(3)
    res_second(1, 3)
    code_far(2)
    res_cores(1, 1)
    res_last(1, 0)
    code_far(3)
    grad_end()
    res_last(1, 1)
    code_done()
    res_done()
    sends_done()


STEP_BLOCKS = 8
CLOSE_STEPS = NBLK // STEP_BLOCKS


def close_kernel(
    resid_ref, cs_ref, dec_ref, dq_in, dk_in, dv_in, gw_in,
    out_ref, dq_ref, dk_ref, dv_ref, gw_ref, layer, copy_sem, out_sem,
):
    copies = [
        pltpu.make_async_copy(src, dst, copy_sem.at[i])
        for i, (src, dst) in enumerate(
            ((dq_in, dq_ref), (dk_in, dk_ref), (dv_in, dv_ref), (gw_in, gw_ref))
        )
    ]
    for copy in copies:
        copy.start()
    depth, width = STEP_BLOCKS * CODE_W, STEP_BLOCKS * BLOCK
    per = CLOSE_STEPS // NZL
    row = lax.broadcasted_iota(jnp.int32, (depth, BLOCK), 0) // CODE_W
    for step in range(CLOSE_STEPS):
        cols = slice(step * width, (step + 1) * width)
        dec = dec_ref[step * depth : (step + 1) * depth, :]
        opened = jnp.concatenate(
            [jnp.where(row == b, dec, jnp.zeros_like(dec)) for b in range(STEP_BLOCKS)], axis=1
        )
        codes = cs_ref[step // per, :, (step % per) * depth : (step % per + 1) * depth]
        added = nn(codes, opened)
        for b in range(SEQ // TB):
            p = place(b)
            rows = slice(b * TB, (b + 1) * TB)
            layer[rows, cols] = (
                resid_ref[rows, cols].astype(F32) + added[p * TB : (p + 1) * TB]
            ).astype(BF)
        copies.append(
            pltpu.make_async_copy(layer.at[:, cols], out_ref.at[:, cols], out_sem.at[step])
        )
        copies[-1].start()
    for copy in copies:
        copy.wait()


def local(queries, key_rows, value_rows, residual_in, out_weight, encoder, decoder, grad_out):
    vmem = pl.BlockSpec(memory_space=pltpu.VMEM)
    anywhere = pl.BlockSpec(memory_space=pl.ANY)
    dec_rows = decoder.reshape(CODE, BLOCK)
    operands = (queries, key_rows, value_rows, residual_in, out_weight, encoder, dec_rows, grad_out)
    operands = [pltpu.with_memory_space_constraint(a, pltpu.HBM) for a in operands]
    resid, code_sum, dq, dk, dv, gw, dec_rows = pl.pallas_call(
        main_kernel,
        out_shape=(
            pltpu.VMEM((SEQ, D), BF),
            pltpu.VMEM((NZL, SEQ, CH), BF),
            pltpu.VMEM((SEQ, AW), BF),
            pltpu.VMEM((SEQ, AW), BF),
            pltpu.VMEM((SEQ, AW), BF),
            pltpu.VMEM((OWN * BLOCK, AW), F32),
            pltpu.VMEM((CODE, BLOCK), BF),
        ),
        in_specs=[anywhere] * 8,
        out_specs=(vmem,) * 7,
        scratch_shapes=[
            pltpu.VMEM((SEQ, AW), BF),
            pltpu.VMEM((SEQ, AW), BF),
            pltpu.VMEM((SEQ, AW), BF),
            pltpu.VMEM((OWN * BLOCK, AW), BF),
            pltpu.VMEM((OWN, CODE_W, BLOCK), BF),
            pltpu.VMEM((TB, D), BF),
            pltpu.VMEM((NZL, CH, AW), BF),
            pltpu.VMEM((NZL, SEQ, CH), BF),
            pltpu.VMEM((SEQ, AW), BF),
            pltpu.VMEM((HEADS, SEQ, SEQ), F32),
            pltpu.VMEM((SEQ, AW), F32),
            pltpu.VMEM((4, HALF, CH), BF),
            pltpu.VMEM((4, HALF, CH), BF),
            pltpu.VMEM((4, HALF, CH), BF),
            pltpu.VMEM((4, HALF, CH), BF),
            pltpu.VMEM((4, PAIR, CH), BF),
            pltpu.VMEM((4, PAIR, CH), BF),
            pltpu.VMEM((4, PAIR, CH), BF),
            pltpu.VMEM((4, PAIR, CH), BF),
            pltpu.VMEM((4, PAIR, CH), BF),
            pltpu.VMEM((4, PAIR, CH), BF),
            pltpu.VMEM((NZL, NX, ER, AW), BF),
            pltpu.VMEM((NZL, ER, AW), BF),
            pltpu.VMEM((NZL, ER, AW), BF),
            pltpu.VMEM((NZL, ER, AW), BF),
            pltpu.VMEM((NZL, ER, AW), BF),
            pltpu.VMEM((NZL, ER, AW), BF),
            pltpu.VMEM((3, ER, AW), BF),
            pltpu.VMEM((ER, AW), BF),
            pltpu.SemaphoreType.DMA((N_SEND,)),
            pltpu.SemaphoreType.DMA((N_RECV,)),
            pltpu.SemaphoreType.DMA((5,)),
            pltpu.SemaphoreType.DMA((NZL,)),
            pltpu.SemaphoreType.DMA((NZL,)),
            pltpu.SemaphoreType.DMA((NZL,)),
            pltpu.SemaphoreType.DMA((8,)),
        ],
        name="exchange",
        compiler_params=pltpu.CompilerParams(
            collective_id=0, has_side_effects=True, vmem_limit_bytes=32 * 2**20
        ),
    )(*operands)

    return pl.pallas_call(
        close_kernel,
        out_shape=(
            pltpu.HBM((SEQ, D), BF),
            pltpu.HBM((SEQ, AW), BF),
            pltpu.HBM((SEQ, AW), BF),
            pltpu.HBM((SEQ, AW), BF),
            pltpu.HBM((OWN * BLOCK, AW), F32),
        ),
        in_specs=[vmem] * 7,
        out_specs=(anywhere,) * 5,
        scratch_shapes=[
            pltpu.VMEM((SEQ, D), BF),
            pltpu.SemaphoreType.DMA((4,)),
            pltpu.SemaphoreType.DMA((CLOSE_STEPS,)),
        ],
        name="close",
        compiler_params=pltpu.CompilerParams(vmem_limit_bytes=20 * 2**20),
    )(resid, code_sum, dec_rows, dq, dk, dv, gw)


def solution(mesh):
    placed = (
        P("dp", "tensor"),
        P("dp", "tensor"),
        P("dp", "tensor"),
        P(("dp", "tensor"), None),
        P("dp", "tensor"),
        P(),
        P(),
        P(("dp", "tensor"), None),
    )
    return jax.shard_map(
        local,
        mesh=mesh,
        in_specs=placed,
        out_specs=(
            P("dp", None),
            P("dp", "tensor"),
            P("dp", "tensor"),
            P("dp", "tensor"),
            P("dp", "tensor"),
        ),
        check_vma=False,
    )
```

```python
import math

import jax
import jax.numpy as jnp
from jax import lax
from jax.experimental import pallas as pl
from jax.experimental.pallas import tpu as pltpu
from jax.sharding import PartitionSpec as P

HD = 128
NEG_FILL = -1e30
MESH = pl.DeviceIdType.MESH
BF, F32 = jnp.bfloat16, jnp.float32

NX, NZL, NY, NZH, NC = 4, 4, 4, 2, 2
TB = 16
SEQ = 256
HEADS = 3
AW = HEADS * HD
NBLK, CODE_W, BLOCK = 96, 32, 128
CODE = NBLK * CODE_W
D = NBLK * BLOCK
OWN = 6
ER = OWN * CODE_W
CH = NX * ER
HALF = SEQ // NC
PAIR = TB * NZH


def nt(a, b):
    return lax.dot_general(a, b, (((1,), (1,)), ((), ())), preferred_element_type=F32)


def nn(a, b):
    return lax.dot_general(a, b, (((1,), (0,)), ((), ())), preferred_element_type=F32)


def tn(a, b):
    return lax.dot_general(a, b, (((0,), (0,)), ((), ())), preferred_element_type=F32)


def place(t):
    return ((t % NC) * NY + t // (NC * NZH)) * NZH + (t // NC) % NZH


N_SEND, N_RECV = 48, 94


class Sems:
    def __init__(self, send, recv):
        self.send, self.recv, self.groups, self.used, self.started = send, recv, {}, 0, []

    def slot(self, group):
        if group not in self.groups:
            self.groups[group] = self.used
            self.used += 1
        return self.recv.at[self.groups[group]]

    def copy(self, src, dst, target, group=None):
        n = len(self.started)
        if n >= N_SEND:
            self.started[n - N_SEND].wait_send()
        made = pltpu.make_async_remote_copy(
            src_ref=src,
            dst_ref=dst,
            send_sem=self.send.at[n % N_SEND],
            recv_sem=self.slot(n if group is None else group),
            device_id=target,
            device_id_type=MESH,
        )
        made.start()
        self.started.append(made)
        return made

    def arrived(self, ref, group, target):
        wait_for(ref, self.send.at[0], self.slot(group), target)

G_ORDER = (1, 3, 2, 0)
STEPS = (1, 3, 2)
PIECES = 4


def wait_for(ref, send_sem, recv_sem, target):
    pltpu.make_async_remote_copy(
        src_ref=ref,
        dst_ref=ref,
        send_sem=send_sem,
        recv_sem=recv_sem,
        device_id=target,
        device_id_type=MESH,
    ).wait_recv()


def main_kernel(
    q_hbm, k_hbm, v_hbm, res_ref, w_hbm, enc_hbm, dec_hbm, go_hbm,
    resid_ref, ag, dq_ref, dk_ref, dv_ref, gw_ref, dec_ref,
    q_ref, k_ref, v_ref, w_ref, enc, go_ref,
    ew, gcb, attn_p, probs, ga,
    c_own, c_send, c_recv, y_sum, y_via, y_mid, y_near, y_far, z_sum, z_recv,
    gp, g_via, g_mid, g_near, g_far, g_sum, gz_recv, gz_via,
    send_sem, recv_sem, line_send, line_recv, gz_send, gz_arrive, local_sem,
):
    dp, t = lax.axis_index("dp"), lax.axis_index("tensor")
    zl, x = dp // NX, dp % NX
    y, zh, c = t // (NZH * NC), (t // NC) % NZH, t % NC

    def to_x(k):
        return (zl * NX + (x + k) % NX, t)

    def to_zl(k):
        return (((zl + k) % NZL) * NX + x, t)

    def to_y(k):
        return (dp, (((y + k) % NY) * NZH + zh) * NC + c)

    to_zh = (dp, (y * NZH + 1 - zh) * NC + c)
    to_c = (dp, (y * NZH + zh) * NC + 1 - c)

    sems = Sems(send_sem, recv_sem)
    send = sems.copy

    barrier = pltpu.get_barrier_semaphore()
    peers = [to_x(1), to_x(3)] + [to_zl(k) for k in STEPS]
    peers += [to_y(1), to_y(3), to_zh, to_c]
    for peer in peers:
        pl.semaphore_signal(barrier, inc=1, device_id=peer, device_id_type=MESH)

    own_rows = pl.ds(pl.multiple_of(t * TB, TB), TB)
    loads = {}
    for i, (name, src, dst) in enumerate((
        ("enc", enc_hbm.at[pl.ds(dp * OWN, OWN)], enc),
        ("w", w_hbm, w_ref),
        ("go", go_hbm, go_ref),
        ("dec", dec_hbm, dec_ref),
        ("q", q_hbm, q_ref),
        ("k", k_hbm, k_ref),
        ("v", v_hbm, v_ref),
        ("res", res_ref, resid_ref.at[own_rows]),
    )):
        loads[name] = pltpu.make_async_copy(src, dst, local_sem.at[i])
        loads[name].start()

    def ew_at(zl_, x_):
        return ew.at[zl_, pl.ds(pl.multiple_of(x_ * ER, ER), ER)]

    loads["enc"].wait()
    loads["w"].wait()
    for b in range(OWN):
        rows = pl.ds(pl.multiple_of(x * ER + b * CODE_W, CODE_W), CODE_W)
        ew[zl, rows, :] = nn(enc[b], w_ref[b * BLOCK : (b + 1) * BLOCK, :]).astype(BF)
    pl.semaphore_wait(barrier, len(peers))

    zls = [zl, zl + 1 - 2 * (zl % 2), 2 - zl // 2, 3 - 3 * (zl // 2)]

    def line_copy(slot, z_, step):
        return pltpu.make_async_remote_copy(
            src_ref=ew_at(z_, x),
            dst_ref=ew_at(z_, x),
            send_sem=line_send.at[slot],
            recv_sem=line_recv.at[z_],
            device_id=((zl + step) * NX + x, t),
            device_id_type=MESH,
        )

    line = [(zl < NZL - 1, 0, zl, 1), (zl > 0, 1, zl, -1)]
    for i in range(1, NZL):
        up = zls[i] < zl
        goes = jnp.logical_or(
            jnp.logical_and(up, zl < NZL - 1), jnp.logical_and(jnp.logical_not(up), zl > 0)
        )
        line.append((goes, 1 + i, zls[i], jnp.where(up, 1, -1)))

    def line_start(goes, *rest):
        @pl.when(goes)
        def _():
            line_copy(*rest).start()

    for entry in line[:2]:
        line_start(*entry)
    e_up, e_down, e_far = {}, {}, {}
    inner = jnp.logical_and(zl > 0, zl < NZL - 1)
    outer = jnp.logical_not(inner)

    def weight_x(i):
        e_up[i] = send(ew_at(zls[i], x), ew_at(zls[i], x), to_x(1))
        e_down[i] = send(ew_at(zls[i], x), ew_at(zls[i], x), to_x(3))

    def weight_x2(i):
        if i % 2 == 0:
            e_up[i].wait_recv()
            at = ew_at(zls[i], (x + 3) % NX)
            e_far[i] = send(at, at, to_x(1))
        else:
            e_down[i].wait_recv()
            at = ew_at(zls[i], (x + 1) % NX)
            e_far[i] = send(at, at, to_x(3))

    weight_x(0)

    def place_of(y_, zh_, c_):
        return (c_ * NY + y_) * NZH + zh_

    def block_rows(p, n=1):
        return pl.ds(pl.multiple_of(p * TB, TB), TB * n)

    mine = block_rows(place_of(y, zh, c))
    other = block_rows(place_of(y, 1 - zh, c))
    lane_block = lax.broadcasted_iota(jnp.int32, (TB, BLOCK), 1) // CODE_W
    loads["res"].wait()
    loads["go"].wait()
    loads["dec"].wait()
    for g in range(NBLK // 4):
        wide = jnp.concatenate(
            [go_ref[:, (4 * g + j) * BLOCK : (4 * g + j + 1) * BLOCK] for j in range(4)], axis=0
        )
        coded = nt(wide, dec_ref[g * BLOCK : (g + 1) * BLOCK, :])
        picked = coded[:TB]
        for j in range(1, 4):
            picked = jnp.where(lane_block == j, coded[j * TB : (j + 1) * TB], picked)
        gcb[g // 6, mine, (g % 6) * BLOCK : (g % 6 + 1) * BLOCK] = picked.astype(BF)

    gc_up, gc_down, gc_far = {}, {}, {}
    gc_z = send(gcb.at[:, mine], gcb.at[:, mine], to_zh)

    def cotangent_first(i):
        at = gcb.at[:, (mine, other)[i]]
        gc_up[i] = send(at, at, to_y(1))
        gc_down[i] = send(at, at, to_y(3))

    def cotangent_core(y_):
        at = gcb.at[:, block_rows(place_of(y_, 0, c), NZH)]
        send(at, at, to_c, "gc")

    def cotangent_y():
        gc_z.wait_recv()
        cotangent_first(1)
        cotangent_core(y)

    def cotangent_relay():
        gc_up[0].wait_recv()
        at = gcb.at[:, block_rows(place_of((y + 3) % NY, zh, c))]
        gc_far[0] = send(at, at, to_y(1))
        gc_down[0].wait_recv()
        gc_down[1].wait_recv()
        at = gcb.at[:, block_rows(place_of((y + 1) % NY, 1 - zh, c))]
        gc_far[1] = send(at, at, to_y(3))
        cotangent_core((y + 1) % NY)
        gc_up[1].wait_recv()
        cotangent_core((y + 3) % NY)

    def cotangent_c():
        gc_far[0].wait_recv()
        gc_far[1].wait_recv()
        cotangent_core((y + 2) % NY)
        sems.arrived(gcb.at[:, :HALF], "gc", to_c)

    cotangent_first(0)

    def res_at(y_, zh_, p):
        rows = pl.ds(pl.multiple_of((y_ * NZH + zh_) * (NC * TB) + c * TB, TB), TB)
        return resid_ref.at[rows, p * (D // PIECES) : (p + 1) * (D // PIECES)]

    res = {}
    shards = (zh, 1 - zh)

    def res_move(name, y_, i, p, target):
        at = res_at(y_, shards[i], p)
        res[name, i, p] = send(at, at, target)

    def res_core(k, i, p, count=1):
        rows = ((y + k) % NY * NZH + shards[i]) * (NC * TB) + c * TB
        width = D // PIECES
        at = resid_ref.at[pl.ds(pl.multiple_of(rows, TB), TB), p * width : (p + count) * width]
        send(at, at, to_c, "res")

    def res_z(p):
        res_move("z", y, 0, p, to_zh)

    def res_first(i, p):
        if i:
            res["z", 0, p].wait_recv()
        res_move("up", y, i, p, to_y(1))
        res_move("down", y, i, p, to_y(3))

    def res_second(i, p):
        res["up", i, p].wait_recv()
        if p % 2 == 0:
            res_move("far", (y + 3) % NY, i, p, to_y(1))
        res["down", i, p].wait_recv()
        if p % 2:
            res_move("far", (y + 1) % NY, i, p, to_y(3))

    def res_cores(i, p, count=1):
        res_core(3, i, p, count)
        res_core(1, i, p, count)

    def res_last(i, p, count=1):
        for q in range(p, p + count):
            res["far", i, q].wait_recv()
        res_core(2, i, p, count)

    scale = 1.0 / math.sqrt(HD)

    def attention_forward():
        grad_slot(1, True)
        grad_slot(3, True)
        for name in "qkv":
            loads[name].wait()
        row_index = lax.broadcasted_iota(jnp.int32, (SEQ, SEQ), 0)
        col_index = lax.broadcasted_iota(jnp.int32, (SEQ, SEQ), 1)
        for h in range(HEADS):
            cols = slice(h * HD, (h + 1) * HD)
            scores = nt(q_ref[:, cols], k_ref[:, cols]) * scale
            scores = jnp.where(col_index <= row_index, scores, NEG_FILL)
            weights = jnp.exp(scores - jnp.max(scores, axis=-1, keepdims=True))
            prob = weights / jnp.sum(weights, axis=-1, keepdims=True)
            probs[h] = prob
            mixed = nn(prob.astype(BF), v_ref[:, cols]).astype(BF)
            for b in range(SEQ // TB):
                p = place(b)
                attn_p[p * TB : (p + 1) * TB, cols] = mixed[b * TB : (b + 1) * TB]

    def attention_backward():
        for h in range(HEADS):
            cols = slice(h * HD, (h + 1) * HD)
            grad = jnp.concatenate(
                [ga[place(b) * TB : (place(b) + 1) * TB, cols] for b in range(SEQ // TB)], axis=0
            ).astype(BF)
            prob = probs[h]
            dprobs = nt(grad, v_ref[:, cols])
            center = jnp.sum(dprobs * prob, axis=-1, keepdims=True)
            grad_scores = (prob * (dprobs - center) * scale).astype(BF)
            dq_ref[:, cols] = nn(grad_scores, k_ref[:, cols]).astype(BF)
            dk_ref[:, cols] = tn(grad_scores, q_ref[:, cols]).astype(BF)
            dv_ref[:, cols] = tn(prob.astype(BF), grad).astype(BF)

    g_up, g_down, g_on = {}, {}, {}

    def grad_start(i):
        z_ = (zl + G_ORDER[i]) % NZL
        term = tn(gcb[z_], attn_p[...])
        for x_ in range(NX):
            gp[i, x_] = term[x_ * ER : (x_ + 1) * ER].astype(BF)
        far = gp.at[i, (x + 2) % NX]
        if i % 2 == 0:
            g_up[i] = send(far, g_via.at[i], to_x(1))
            g_down[i] = send(gp.at[i, (x + 3) % NX], g_near.at[i], to_x(3))
        else:
            g_down[i] = send(far, g_via.at[i], to_x(3))
            g_up[i] = send(gp.at[i, (x + 1) % NX], g_near.at[i], to_x(1))

    def grad_on(i):
        step = 1 if i % 2 == 0 else 3
        (g_up if i % 2 == 0 else g_down)[i].wait_recv()
        g_mid[i] = (gp[i, (x + step) % NX].astype(F32) + g_via[i].astype(F32)).astype(BF)
        g_on[i] = send(g_mid.at[i], g_far.at[i], to_x(step))

    def grad_z(i):
        (g_down if i % 2 == 0 else g_up)[i].wait_recv()
        g_on[i].wait_recv()
        total = gp[i, x].astype(F32) + g_near[i].astype(F32) + g_far[i].astype(F32)
        g_sum[i] = total.astype(BF)
        k = G_ORDER[i]
        if k == 2:
            @pl.when(inner)
            def _():
                wait_for(gz_via, gz_send.at[0], gz_arrive.at[3], to_zl(1))
                g_sum[i] = (total + gz_via[...].astype(F32)).astype(BF)

        if k:
            ends = zl == (-1, NZL - 1, -1, 0)[k]
            step = {1: -1, 3: 1, 2: 0}[k]

            @pl.when(jnp.logical_not(ends))
            def _():
                grad_copy(i, gz_recv.at[k - 1], k - 1, to_zl(k)).start()

            @pl.when(ends)
            def _():
                grad_copy(i, gz_via, 3, ((zl + step) * NX + x, t)).start()


    def grad_copy(i, dst, slot, target):
        return pltpu.make_async_remote_copy(
            src_ref=g_sum.at[i],
            dst_ref=dst,
            send_sem=gz_send.at[i],
            recv_sem=gz_arrive.at[slot],
            device_id=target,
            device_id_type=MESH,
        )

    def grad_slot(k, first):
        lone = zl == {1: 0, 2: -1, 3: NZL - 1}[k]

        @pl.when(lone if first else jnp.logical_not(lone))
        def _():
            if first:
                gz_recv[k - 1] = jnp.zeros((ER, AW), BF)
            else:
                wait_for(gz_recv.at[k - 1], gz_send.at[0], gz_arrive.at[k - 1], to_zl(1))

    def grad_end():
        total = g_sum[G_ORDER.index(0)].astype(F32)
        for k in STEPS:
            grad_slot(k, False)
            total += gz_recv[k - 1].astype(F32)
        summed = total.astype(BF)
        for b in range(OWN):
            gw_ref[b * BLOCK : (b + 1) * BLOCK, :] = tn(
                enc[b], summed[b * CODE_W : (b + 1) * CODE_W]
            )

    c_cp, y_cp, z_cp, a_cp = {}, {}, {}, {}

    def code(i):
        (e_down if i % 2 == 0 else e_up)[i].wait_recv()
        e_far[i].wait_recv()
        codes = nt(attn_p[...], ew[zls[i]]).astype(BF)
        for half in range(NC):
            part = codes[half * HALF : (half + 1) * HALF]

            @pl.when(c == half)
            def _():
                c_own[i] = part

            @pl.when(c != half)
            def _():
                c_send[i] = part

        c_cp[i] = send(c_send.at[i], c_recv.at[i], to_c)

    def grad_attn(i):
        grown = nn(gcb[zls[i]], ew[zls[i]])
        if i == 0:
            ga[...] = grown
        else:
            ga[...] += grown

    def y_block(i, k):
        return y_sum.at[i, pl.ds(pl.multiple_of(((y + k) % NY) * PAIR, PAIR), PAIR)]

    def code_y(i):
        c_cp[i].wait_recv()
        y_sum[i] = (c_own[i].astype(F32) + c_recv[i].astype(F32)).astype(BF)
        step = 1 if i % 2 == 0 else 3
        y_cp[i, "via"] = send(y_block(i, 2), y_via.at[i], to_y(step))
        y_cp[i, "near"] = send(y_block(i, 4 - step), y_near.at[i], to_y(4 - step))

    def code_mid(i):
        step = 1 if i % 2 == 0 else 3
        y_cp[i, "via"].wait_recv()
        y_mid[i] = (y_block(i, step)[...].astype(F32) + y_via[i].astype(F32)).astype(BF)
        y_cp[i, "far"] = send(y_mid.at[i], y_far.at[i], to_y(step))

    def code_z(i):
        y_cp[i, "near"].wait_recv()
        y_cp[i, "far"].wait_recv()
        total = y_block(i, 0)[...].astype(F32) + y_near[i].astype(F32) + y_far[i].astype(F32)
        z_sum[i] = total.astype(BF)
        z_cp[i] = send(z_sum.at[i], z_recv.at[i], to_zh)

    def ag_at(z_, y_):
        return ag.at[z_, pl.ds(pl.multiple_of((c * NY + y_) * PAIR, PAIR), PAIR)]

    def code_back(i):
        z_cp[i].wait_recv()
        at = ag_at(zls[i], y)
        at[...] = (z_sum[i].astype(F32) + z_recv[i].astype(F32)).astype(BF)
        a_cp[i, "up"] = send(at, at, to_y(1))
        a_cp[i, "down"] = send(at, at, to_y(3))
        send(at, at, to_c, "ag")

    def code_out(i):
        for name, k in (("up", 3), ("down", 1)):
            a_cp[i, name].wait_recv()
            at = ag_at(zls[i], (y + k) % NY)
            if name == ("up", "down")[i % 2]:
                a_cp[i, "far"] = send(at, at, to_y(4 - k))
            send(at, at, to_c, "ag")

    def code_far(i):
        a_cp[i, "far"].wait_recv()
        at = ag_at(zls[i], (y + 2) % NY)
        send(at, at, to_c, "ag")

    def code_done():
        sems.arrived(ag.at[:, :HALF], "ag", to_c)

    def res_done():
        sems.arrived(resid_ref.at[:HALF], "res", to_c)

    def sends_done():
        for goes, *rest in line:

            @pl.when(goes)
            def _():
                line_copy(*rest).wait_send()

        for i in range(NZL):
            if G_ORDER[i]:
                grad_copy(i, gz_recv.at[0], 0, to_zl(1)).wait_send()
        for made in sems.started[-N_SEND:]:
            made.wait_send()

    def weight_z(i):
        weight_line(i)
        weight_x(i)

    def weight_line(i):
        at = ew_at(zls[i], x)
        wait_for(at, line_send.at[0], line_recv.at[zls[i]], to_zl(1))
        line_start(*line[1 + i])

    def weight_last(here):
        @pl.when(here)
        def _():
            weight_line(NZL - 1)

    for p in range(PIECES - 1):
        res_first(0, p)
    attention_forward()
    weight_x2(0)
    weight_z(1)
    weight_z(2)
    code(0)
    weight_last(inner)
    weight_x2(1)
    cotangent_y()
    code_y(0)
    weight_last(outer)
    weight_x(3)
    res_z(0)
    weight_x2(2)
    res_z(1)
    cotangent_relay()
    res_first(0, 3)
    code_mid(0)
    res_second(0, 0)
    res_second(0, 1)
    res_core(0, 0, 0, 4)
    res_cores(0, 0, 2)
    code(1)
    code_y(1)
    weight_x2(3)
    res_second(0, 2)
    res_z(2)
    code(2)
    cotangent_c()
    grad_start(0)
    grad_start(1)
    code_mid(1)
    code_y(2)
    res_first(1, 0)
    code_z(0)
    res_z(3)
    code(3)
    code_y(3)
    res_second(0, 3)
    res_cores(0, 2, 2)
    grad_start(2)
    code_z(1)
    code_mid(2)
    res_first(1, 1)
    grad_on(0)
    res_core(0, 1, 0, 2)
    grad_start(3)
    grad_attn(0)
    grad_attn(1)
    grad_attn(2)
    grad_attn(3)
    res_last(0, 0, 2)
    res_first(1, 2)
    code_mid(3)
    grad_on(1)
    code_back(0)
    code_z(2)
    attention_backward()
    grad_on(2)
    grad_z(0)
    grad_on(3)
    res_first(1, 3)
    res_core(0, 1, 2, 2)
    code_z(3)
    code_back(1)
    code_out(0)
    grad_z(1)
    res_second(1, 0)
    res_second(1, 1)
    res_cores(1, 0, 2)
    res_last(0, 2, 2)
    code_back(2)
    grad_z(3)
    code_out(1)
    code_back(3)
    res_second(1, 2)
    grad_z(2)
    code_out(2)
    code_far(0)
    res_second(1, 3)
    res_cores(1, 2)
    code_out(3)
    code_far(1)
    res_last(1, 0)
    res_last(1, 1)
    res_cores(1, 3)
    code_far(2)
    code_far(3)
    res_last(1, 2)
    grad_end()
    res_last(1, 3)
    code_done()
    res_done()
    sends_done()


STEP_BLOCKS = 8
CLOSE_STEPS = NBLK // STEP_BLOCKS


def close_kernel(
    resid_ref, cs_ref, dec_ref, dq_in, dk_in, dv_in, gw_in,
    out_ref, dq_ref, dk_ref, dv_ref, gw_ref, layer, copy_sem, out_sem,
):
    copies = [
        pltpu.make_async_copy(src, dst, copy_sem.at[i])
        for i, (src, dst) in enumerate(
            ((dq_in, dq_ref), (dk_in, dk_ref), (dv_in, dv_ref), (gw_in, gw_ref))
        )
    ]
    for copy in copies:
        copy.start()
    depth, width = STEP_BLOCKS * CODE_W, STEP_BLOCKS * BLOCK
    per = CLOSE_STEPS // NZL
    row = lax.broadcasted_iota(jnp.int32, (depth, BLOCK), 0) // CODE_W
    for step in range(CLOSE_STEPS):
        cols = slice(step * width, (step + 1) * width)
        dec = dec_ref[step * depth : (step + 1) * depth, :]
        opened = jnp.concatenate(
            [jnp.where(row == b, dec, jnp.zeros_like(dec)) for b in range(STEP_BLOCKS)], axis=1
        )
        codes = cs_ref[step // per, :, (step % per) * depth : (step % per + 1) * depth]
        added = nn(codes, opened)
        for b in range(SEQ // TB):
            p = place(b)
            rows = slice(b * TB, (b + 1) * TB)
            layer[rows, cols] = (
                resid_ref[rows, cols].astype(F32) + added[p * TB : (p + 1) * TB]
            ).astype(BF)
        copies.append(
            pltpu.make_async_copy(layer.at[:, cols], out_ref.at[:, cols], out_sem.at[step])
        )
        copies[-1].start()
    for copy in copies:
        copy.wait()


def local(queries, key_rows, value_rows, residual_in, out_weight, encoder, decoder, grad_out):
    vmem = pl.BlockSpec(memory_space=pltpu.VMEM)
    anywhere = pl.BlockSpec(memory_space=pl.ANY)
    dec_rows = decoder.reshape(CODE, BLOCK)
    operands = (queries, key_rows, value_rows, residual_in, out_weight, encoder, dec_rows, grad_out)
    operands = [pltpu.with_memory_space_constraint(a, pltpu.HBM) for a in operands]
    resid, code_sum, dq, dk, dv, gw, dec_rows = pl.pallas_call(
        main_kernel,
        out_shape=(
            pltpu.VMEM((SEQ, D), BF),
            pltpu.VMEM((NZL, SEQ, CH), BF),
            pltpu.VMEM((SEQ, AW), BF),
            pltpu.VMEM((SEQ, AW), BF),
            pltpu.VMEM((SEQ, AW), BF),
            pltpu.VMEM((OWN * BLOCK, AW), F32),
            pltpu.VMEM((CODE, BLOCK), BF),
        ),
        in_specs=[anywhere] * 8,
        out_specs=(vmem,) * 7,
        scratch_shapes=[
            pltpu.VMEM((SEQ, AW), BF),
            pltpu.VMEM((SEQ, AW), BF),
            pltpu.VMEM((SEQ, AW), BF),
            pltpu.VMEM((OWN * BLOCK, AW), BF),
            pltpu.VMEM((OWN, CODE_W, BLOCK), BF),
            pltpu.VMEM((TB, D), BF),
            pltpu.VMEM((NZL, CH, AW), BF),
            pltpu.VMEM((NZL, SEQ, CH), BF),
            pltpu.VMEM((SEQ, AW), BF),
            pltpu.VMEM((HEADS, SEQ, SEQ), F32),
            pltpu.VMEM((SEQ, AW), F32),
            pltpu.VMEM((4, HALF, CH), BF),
            pltpu.VMEM((4, HALF, CH), BF),
            pltpu.VMEM((4, HALF, CH), BF),
            pltpu.VMEM((4, HALF, CH), BF),
            pltpu.VMEM((4, PAIR, CH), BF),
            pltpu.VMEM((4, PAIR, CH), BF),
            pltpu.VMEM((4, PAIR, CH), BF),
            pltpu.VMEM((4, PAIR, CH), BF),
            pltpu.VMEM((4, PAIR, CH), BF),
            pltpu.VMEM((4, PAIR, CH), BF),
            pltpu.VMEM((NZL, NX, ER, AW), BF),
            pltpu.VMEM((NZL, ER, AW), BF),
            pltpu.VMEM((NZL, ER, AW), BF),
            pltpu.VMEM((NZL, ER, AW), BF),
            pltpu.VMEM((NZL, ER, AW), BF),
            pltpu.VMEM((NZL, ER, AW), BF),
            pltpu.VMEM((3, ER, AW), BF),
            pltpu.VMEM((ER, AW), BF),
            pltpu.SemaphoreType.DMA((N_SEND,)),
            pltpu.SemaphoreType.DMA((N_RECV,)),
            pltpu.SemaphoreType.DMA((5,)),
            pltpu.SemaphoreType.DMA((NZL,)),
            pltpu.SemaphoreType.DMA((NZL,)),
            pltpu.SemaphoreType.DMA((NZL,)),
            pltpu.SemaphoreType.DMA((8,)),
        ],
        name="exchange",
        compiler_params=pltpu.CompilerParams(
            collective_id=0, has_side_effects=True, vmem_limit_bytes=32 * 2**20
        ),
    )(*operands)

    return pl.pallas_call(
        close_kernel,
        out_shape=(
            pltpu.HBM((SEQ, D), BF),
            pltpu.HBM((SEQ, AW), BF),
            pltpu.HBM((SEQ, AW), BF),
            pltpu.HBM((SEQ, AW), BF),
            pltpu.HBM((OWN * BLOCK, AW), F32),
        ),
        in_specs=[vmem] * 7,
        out_specs=(anywhere,) * 5,
        scratch_shapes=[
            pltpu.VMEM((SEQ, D), BF),
            pltpu.SemaphoreType.DMA((4,)),
            pltpu.SemaphoreType.DMA((CLOSE_STEPS,)),
        ],
        name="close",
        compiler_params=pltpu.CompilerParams(vmem_limit_bytes=20 * 2**20),
    )(resid, code_sum, dec_rows, dq, dk, dv, gw)


def solution(mesh):
    placed = (
        P("dp", "tensor"),
        P("dp", "tensor"),
        P("dp", "tensor"),
        P(("dp", "tensor"), None),
        P("dp", "tensor"),
        P(),
        P(),
        P(("dp", "tensor"), None),
    )
    return jax.shard_map(
        local,
        mesh=mesh,
        in_specs=placed,
        out_specs=(
            P("dp", None),
            P("dp", "tensor"),
            P("dp", "tensor"),
            P("dp", "tensor"),
            P("dp", "tensor"),
        ),
        check_vma=False,
    )
```

```python
import math

import jax
import jax.numpy as jnp
from jax import lax
from jax.experimental import pallas as pl
from jax.experimental.pallas import tpu as pltpu
from jax.sharding import PartitionSpec as P

HD = 128
NEG_FILL = -1e30
MESH = pl.DeviceIdType.MESH
BF, F32 = jnp.bfloat16, jnp.float32

NX, NZL, NY, NZH, NC = 4, 4, 4, 2, 2
TB = 16
SEQ = 256
HEADS = 3
AW = HEADS * HD
NBLK, CODE_W, BLOCK = 96, 32, 128
CODE = NBLK * CODE_W
D = NBLK * BLOCK
OWN = 6
ER = OWN * CODE_W
CH = NX * ER
HALF = SEQ // NC
PAIR = TB * NZH


def nt(a, b):
    return lax.dot_general(a, b, (((1,), (1,)), ((), ())), preferred_element_type=F32)


def nn(a, b):
    return lax.dot_general(a, b, (((1,), (0,)), ((), ())), preferred_element_type=F32)


def tn(a, b):
    return lax.dot_general(a, b, (((0,), (0,)), ((), ())), preferred_element_type=F32)


def place(t):
    return ((t % NC) * NY + t // (NC * NZH)) * NZH + (t // NC) % NZH


KINDS = ("ew", "gc", "res", "grad", "code", "back")
N_RECV = 94


class Sems:
    def __init__(self, send, recv):
        self.send, self.recv, self.groups, self.used, self.started = send, recv, {}, 0, []

    def slot(self, group):
        if group not in self.groups:
            self.groups[group] = self.used
            self.used += 1
        return self.recv.at[self.groups[group]]

    def copy(self, kind, src, dst, target, group=None):
        made = pltpu.make_async_remote_copy(
            src_ref=src,
            dst_ref=dst,
            send_sem=self.send.at[KINDS.index(kind)],
            recv_sem=self.slot(len(self.started) if group is None else group),
            device_id=target,
            device_id_type=MESH,
        )
        made.start()
        self.started.append(made)
        return made

    def sent(self, kind, ref, target):
        pltpu.make_async_remote_copy(
            src_ref=ref,
            dst_ref=ref,
            send_sem=self.send.at[KINDS.index(kind)],
            recv_sem=self.recv.at[0],
            device_id=target,
            device_id_type=MESH,
        ).wait_send()

    def arrived(self, ref, group, target):
        wait_for(ref, self.send.at[0], self.slot(group), target)

G_ORDER = (1, 3, 2, 0)
STEPS = (1, 3, 2)
PIECES = 4


def wait_for(ref, send_sem, recv_sem, target):
    pltpu.make_async_remote_copy(
        src_ref=ref,
        dst_ref=ref,
        send_sem=send_sem,
        recv_sem=recv_sem,
        device_id=target,
        device_id_type=MESH,
    ).wait_recv()


def main_kernel(
    q_hbm, k_hbm, v_hbm, res_ref, w_hbm, enc_hbm, dec_hbm, go_hbm,
    resid_ref, ag, dq_ref, dk_ref, dv_ref, gw_ref, dec_ref,
    q_ref, k_ref, v_ref, w_ref, enc, go_ref,
    ew, gcb, attn_p, probs, ga,
    c_own, c_send, c_recv, y_sum, y_via, y_mid, y_near, y_far, z_sum, z_recv,
    gp, g_via, g_mid, g_near, g_far, g_sum, gz_recv, gz_via,
    send_sem, recv_sem, line_send, line_recv, gz_send, gz_arrive, local_sem,
):
    dp, t = lax.axis_index("dp"), lax.axis_index("tensor")
    zl, x = dp // NX, dp % NX
    y, zh, c = t // (NZH * NC), (t // NC) % NZH, t % NC

    def to_x(k):
        return (zl * NX + (x + k) % NX, t)

    def to_zl(k):
        return (((zl + k) % NZL) * NX + x, t)

    def to_y(k):
        return (dp, (((y + k) % NY) * NZH + zh) * NC + c)

    to_zh = (dp, (y * NZH + 1 - zh) * NC + c)
    to_c = (dp, (y * NZH + zh) * NC + 1 - c)

    sems = Sems(send_sem, recv_sem)
    send = sems.copy

    barrier = pltpu.get_barrier_semaphore()
    peers = [to_x(1), to_x(3)] + [to_zl(k) for k in STEPS]
    peers += [to_y(1), to_y(3), to_zh, to_c]
    for peer in peers:
        pl.semaphore_signal(barrier, inc=1, device_id=peer, device_id_type=MESH)

    own_rows = pl.ds(pl.multiple_of(t * TB, TB), TB)
    loads = {}
    for i, (name, src, dst) in enumerate((
        ("enc", enc_hbm.at[pl.ds(dp * OWN, OWN)], enc),
        ("w", w_hbm, w_ref),
        ("go", go_hbm, go_ref),
        ("dec", dec_hbm, dec_ref),
        ("q", q_hbm, q_ref),
        ("k", k_hbm, k_ref),
        ("v", v_hbm, v_ref),
        ("res", res_ref, resid_ref.at[own_rows]),
    )):
        loads[name] = pltpu.make_async_copy(src, dst, local_sem.at[i])
        loads[name].start()

    def ew_at(zl_, x_):
        return ew.at[zl_, pl.ds(pl.multiple_of(x_ * ER, ER), ER)]

    loads["enc"].wait()
    loads["w"].wait()
    for b in range(OWN):
        rows = pl.ds(pl.multiple_of(x * ER + b * CODE_W, CODE_W), CODE_W)
        ew[zl, rows, :] = nn(enc[b], w_ref[b * BLOCK : (b + 1) * BLOCK, :]).astype(BF)
    pl.semaphore_wait(barrier, len(peers))

    zls = [zl, zl + 1 - 2 * (zl % 2), 2 - zl // 2, 3 - 3 * (zl // 2)]

    def line_copy(slot, z_, step):
        return pltpu.make_async_remote_copy(
            src_ref=ew_at(z_, x),
            dst_ref=ew_at(z_, x),
            send_sem=line_send.at[slot],
            recv_sem=line_recv.at[z_],
            device_id=((zl + step) * NX + x, t),
            device_id_type=MESH,
        )

    line = [(zl < NZL - 1, 0, zl, 1), (zl > 0, 1, zl, -1)]
    for i in range(1, NZL):
        up = zls[i] < zl
        goes = jnp.logical_or(
            jnp.logical_and(up, zl < NZL - 1), jnp.logical_and(jnp.logical_not(up), zl > 0)
        )
        line.append((goes, 1 + i, zls[i], jnp.where(up, 1, -1)))

    def line_start(goes, *rest):
        @pl.when(goes)
        def _():
            line_copy(*rest).start()

    for entry in line[:2]:
        line_start(*entry)
    e_up, e_down, e_far = {}, {}, {}
    inner = jnp.logical_and(zl > 0, zl < NZL - 1)
    outer = jnp.logical_not(inner)

    def weight_x(i):
        e_up[i] = send("ew", ew_at(zls[i], x), ew_at(zls[i], x), to_x(1))
        e_down[i] = send("ew", ew_at(zls[i], x), ew_at(zls[i], x), to_x(3))

    def weight_x2(i):
        if i % 2 == 0:
            e_up[i].wait_recv()
            at = ew_at(zls[i], (x + 3) % NX)
            e_far[i] = send("ew", at, at, to_x(1))
        else:
            e_down[i].wait_recv()
            at = ew_at(zls[i], (x + 1) % NX)
            e_far[i] = send("ew", at, at, to_x(3))

    weight_x(0)

    def place_of(y_, zh_, c_):
        return (c_ * NY + y_) * NZH + zh_

    def block_rows(p, n=1):
        return pl.ds(pl.multiple_of(p * TB, TB), TB * n)

    mine = block_rows(place_of(y, zh, c))
    other = block_rows(place_of(y, 1 - zh, c))
    lane_block = lax.broadcasted_iota(jnp.int32, (TB, BLOCK), 1) // CODE_W
    loads["res"].wait()
    loads["go"].wait()
    loads["dec"].wait()
    for g in range(NBLK // 4):
        wide = jnp.concatenate(
            [go_ref[:, (4 * g + j) * BLOCK : (4 * g + j + 1) * BLOCK] for j in range(4)], axis=0
        )
        coded = nt(wide, dec_ref[g * BLOCK : (g + 1) * BLOCK, :])
        picked = coded[:TB]
        for j in range(1, 4):
            picked = jnp.where(lane_block == j, coded[j * TB : (j + 1) * TB], picked)
        gcb[g // 6, mine, (g % 6) * BLOCK : (g % 6 + 1) * BLOCK] = picked.astype(BF)

    gc_up, gc_down, gc_far = {}, {}, {}
    gc_z = send("gc", gcb.at[:, mine], gcb.at[:, mine], to_zh)

    def cotangent_first(i):
        at = gcb.at[:, (mine, other)[i]]
        gc_up[i] = send("gc", at, at, to_y(1))
        gc_down[i] = send("gc", at, at, to_y(3))

    def cotangent_core(y_):
        at = gcb.at[:, block_rows(place_of(y_, 0, c), NZH)]
        send("gc", at, at, to_c, "gc")

    def cotangent_y():
        gc_z.wait_recv()
        cotangent_first(1)
        cotangent_core(y)

    def cotangent_relay():
        gc_up[0].wait_recv()
        at = gcb.at[:, block_rows(place_of((y + 3) % NY, zh, c))]
        gc_far[0] = send("gc", at, at, to_y(1))
        gc_down[0].wait_recv()
        gc_down[1].wait_recv()
        at = gcb.at[:, block_rows(place_of((y + 1) % NY, 1 - zh, c))]
        gc_far[1] = send("gc", at, at, to_y(3))
        cotangent_core((y + 1) % NY)
        gc_up[1].wait_recv()
        cotangent_core((y + 3) % NY)

    def cotangent_c():
        gc_far[0].wait_recv()
        gc_far[1].wait_recv()
        cotangent_core((y + 2) % NY)
        sems.arrived(gcb.at[:, :HALF], "gc", to_c)

    cotangent_first(0)

    def res_at(y_, zh_, p):
        rows = pl.ds(pl.multiple_of((y_ * NZH + zh_) * (NC * TB) + c * TB, TB), TB)
        return resid_ref.at[rows, p * (D // PIECES) : (p + 1) * (D // PIECES)]

    res = {}
    shards = (zh, 1 - zh)

    def res_move(name, y_, i, p, target):
        at = res_at(y_, shards[i], p)
        res[name, i, p] = send("res", at, at, target)

    def res_core(k, i, p, count=1):
        rows = ((y + k) % NY * NZH + shards[i]) * (NC * TB) + c * TB
        width = D // PIECES
        at = resid_ref.at[pl.ds(pl.multiple_of(rows, TB), TB), p * width : (p + count) * width]
        send("res", at, at, to_c, "res")

    def res_z(p):
        res_move("z", y, 0, p, to_zh)

    def res_first(i, p):
        if i:
            res["z", 0, p].wait_recv()
        res_move("up", y, i, p, to_y(1))
        res_move("down", y, i, p, to_y(3))

    def res_second(i, p):
        res["up", i, p].wait_recv()
        if p % 2 == 0:
            res_move("far", (y + 3) % NY, i, p, to_y(1))
        res["down", i, p].wait_recv()
        if p % 2:
            res_move("far", (y + 1) % NY, i, p, to_y(3))

    def res_cores(i, p, count=1):
        res_core(3, i, p, count)
        res_core(1, i, p, count)

    def res_last(i, p, count=1):
        for q in range(p, p + count):
            res["far", i, q].wait_recv()
        res_core(2, i, p, count)

    scale = 1.0 / math.sqrt(HD)

    def attention_forward():
        grad_slot(1, True)
        grad_slot(3, True)
        for name in "qkv":
            loads[name].wait()
        row_index = lax.broadcasted_iota(jnp.int32, (SEQ, SEQ), 0)
        col_index = lax.broadcasted_iota(jnp.int32, (SEQ, SEQ), 1)
        for h in range(HEADS):
            cols = slice(h * HD, (h + 1) * HD)
            scores = nt(q_ref[:, cols], k_ref[:, cols]) * scale
            scores = jnp.where(col_index <= row_index, scores, NEG_FILL)
            weights = jnp.exp(scores - jnp.max(scores, axis=-1, keepdims=True))
            prob = weights / jnp.sum(weights, axis=-1, keepdims=True)
            probs[h] = prob
            mixed = nn(prob.astype(BF), v_ref[:, cols]).astype(BF)
            for b in range(SEQ // TB):
                p = place(b)
                attn_p[p * TB : (p + 1) * TB, cols] = mixed[b * TB : (b + 1) * TB]

    def attention_backward():
        for h in range(HEADS):
            cols = slice(h * HD, (h + 1) * HD)
            grad = jnp.concatenate(
                [ga[place(b) * TB : (place(b) + 1) * TB, cols] for b in range(SEQ // TB)], axis=0
            ).astype(BF)
            prob = probs[h]
            dprobs = nt(grad, v_ref[:, cols])
            center = jnp.sum(dprobs * prob, axis=-1, keepdims=True)
            grad_scores = (prob * (dprobs - center) * scale).astype(BF)
            dq_ref[:, cols] = nn(grad_scores, k_ref[:, cols]).astype(BF)
            dk_ref[:, cols] = tn(grad_scores, q_ref[:, cols]).astype(BF)
            dv_ref[:, cols] = tn(prob.astype(BF), grad).astype(BF)

    g_up, g_down, g_on = {}, {}, {}

    def grad_start(i):
        z_ = (zl + G_ORDER[i]) % NZL
        term = tn(gcb[z_], attn_p[...])
        for x_ in range(NX):
            gp[i, x_] = term[x_ * ER : (x_ + 1) * ER].astype(BF)
        far = gp.at[i, (x + 2) % NX]
        if i % 2 == 0:
            g_up[i] = send("grad", far, g_via.at[i], to_x(1))
            g_down[i] = send("grad", gp.at[i, (x + 3) % NX], g_near.at[i], to_x(3))
        else:
            g_down[i] = send("grad", far, g_via.at[i], to_x(3))
            g_up[i] = send("grad", gp.at[i, (x + 1) % NX], g_near.at[i], to_x(1))

    def grad_on(i):
        step = 1 if i % 2 == 0 else 3
        (g_up if i % 2 == 0 else g_down)[i].wait_recv()
        g_mid[i] = (gp[i, (x + step) % NX].astype(F32) + g_via[i].astype(F32)).astype(BF)
        g_on[i] = send("grad", g_mid.at[i], g_far.at[i], to_x(step))

    def grad_z(i):
        (g_down if i % 2 == 0 else g_up)[i].wait_recv()
        g_on[i].wait_recv()
        total = gp[i, x].astype(F32) + g_near[i].astype(F32) + g_far[i].astype(F32)
        g_sum[i] = total.astype(BF)
        k = G_ORDER[i]
        if k == 2:
            @pl.when(inner)
            def _():
                wait_for(gz_via, gz_send.at[0], gz_arrive.at[3], to_zl(1))
                g_sum[i] = (total + gz_via[...].astype(F32)).astype(BF)

        if k:
            ends = zl == (-1, NZL - 1, -1, 0)[k]
            step = {1: -1, 3: 1, 2: 0}[k]

            @pl.when(jnp.logical_not(ends))
            def _():
                grad_copy(i, gz_recv.at[k - 1], k - 1, to_zl(k)).start()

            @pl.when(ends)
            def _():
                grad_copy(i, gz_via, 3, ((zl + step) * NX + x, t)).start()


    def grad_copy(i, dst, slot, target):
        return pltpu.make_async_remote_copy(
            src_ref=g_sum.at[i],
            dst_ref=dst,
            send_sem=gz_send.at[i],
            recv_sem=gz_arrive.at[slot],
            device_id=target,
            device_id_type=MESH,
        )

    def grad_slot(k, first):
        lone = zl == {1: 0, 2: -1, 3: NZL - 1}[k]

        @pl.when(lone if first else jnp.logical_not(lone))
        def _():
            if first:
                gz_recv[k - 1] = jnp.zeros((ER, AW), BF)
            else:
                wait_for(gz_recv.at[k - 1], gz_send.at[0], gz_arrive.at[k - 1], to_zl(1))

    def grad_end():
        total = g_sum[G_ORDER.index(0)].astype(F32)
        for k in STEPS:
            grad_slot(k, False)
            total += gz_recv[k - 1].astype(F32)
        summed = total.astype(BF)
        for b in range(OWN):
            gw_ref[b * BLOCK : (b + 1) * BLOCK, :] = tn(
                enc[b], summed[b * CODE_W : (b + 1) * CODE_W]
            )

    c_cp, y_cp, z_cp, a_cp = {}, {}, {}, {}

    def code(i):
        (e_down if i % 2 == 0 else e_up)[i].wait_recv()
        e_far[i].wait_recv()
        codes = nt(attn_p[...], ew[zls[i]]).astype(BF)
        for half in range(NC):
            part = codes[half * HALF : (half + 1) * HALF]

            @pl.when(c == half)
            def _():
                c_own[i] = part

            @pl.when(c != half)
            def _():
                c_send[i] = part

        c_cp[i] = send("code", c_send.at[i], c_recv.at[i], to_c)

    def grad_attn(i):
        grown = nn(gcb[zls[i]], ew[zls[i]])
        if i == 0:
            ga[...] = grown
        else:
            ga[...] += grown

    def y_block(i, k):
        return y_sum.at[i, pl.ds(pl.multiple_of(((y + k) % NY) * PAIR, PAIR), PAIR)]

    def code_y(i):
        c_cp[i].wait_recv()
        y_sum[i] = (c_own[i].astype(F32) + c_recv[i].astype(F32)).astype(BF)
        step = 1 if i % 2 == 0 else 3
        y_cp[i, "via"] = send("code", y_block(i, 2), y_via.at[i], to_y(step))
        y_cp[i, "near"] = send("code", y_block(i, 4 - step), y_near.at[i], to_y(4 - step))

    def code_mid(i):
        step = 1 if i % 2 == 0 else 3
        y_cp[i, "via"].wait_recv()
        y_mid[i] = (y_block(i, step)[...].astype(F32) + y_via[i].astype(F32)).astype(BF)
        y_cp[i, "far"] = send("code", y_mid.at[i], y_far.at[i], to_y(step))

    def code_z(i):
        y_cp[i, "near"].wait_recv()
        y_cp[i, "far"].wait_recv()
        total = y_block(i, 0)[...].astype(F32) + y_near[i].astype(F32) + y_far[i].astype(F32)
        z_sum[i] = total.astype(BF)
        z_cp[i] = send("code", z_sum.at[i], z_recv.at[i], to_zh)

    def ag_at(z_, y_):
        return ag.at[z_, pl.ds(pl.multiple_of((c * NY + y_) * PAIR, PAIR), PAIR)]

    def code_back(i):
        z_cp[i].wait_recv()
        at = ag_at(zls[i], y)
        at[...] = (z_sum[i].astype(F32) + z_recv[i].astype(F32)).astype(BF)
        a_cp[i, "up"] = send("back", at, at, to_y(1))
        a_cp[i, "down"] = send("back", at, at, to_y(3))
        send("back", at, at, to_c, "ag")

    def code_out(i):
        for name, k in (("up", 3), ("down", 1)):
            a_cp[i, name].wait_recv()
            at = ag_at(zls[i], (y + k) % NY)
            if name == ("up", "down")[i % 2]:
                a_cp[i, "far"] = send("back", at, at, to_y(4 - k))
            send("back", at, at, to_c, "ag")

    def code_far(i):
        a_cp[i, "far"].wait_recv()
        at = ag_at(zls[i], (y + 2) % NY)
        send("back", at, at, to_c, "ag")

    def code_done():
        sems.arrived(ag.at[:, :HALF], "ag", to_c)

    def res_done():
        sems.arrived(resid_ref.at[:HALF], "res", to_c)

    def sends_done():
        for goes, *rest in line:

            @pl.when(goes)
            def _():
                line_copy(*rest).wait_send()

        for i in range(NZL):
            if G_ORDER[i]:
                grad_copy(i, gz_recv.at[0], 0, to_zl(1)).wait_send()
        sems.sent("ew", ew.at[:3], to_c)
        sems.sent("gc", gcb.at[:, : SEQ - TB], to_c)
        sems.sent("res", resid_ref.at[: SEQ - TB], to_c)
        sems.sent("grad", gp.at[:3], to_c)
        sems.sent("code", ag, to_c)
        sems.sent("back", ag.at[:, : SEQ - PAIR], to_c)

    def weight_z(i):
        weight_line(i)
        weight_x(i)

    def weight_line(i):
        at = ew_at(zls[i], x)
        wait_for(at, line_send.at[0], line_recv.at[zls[i]], to_zl(1))
        line_start(*line[1 + i])

    def weight_last(here):
        @pl.when(here)
        def _():
            weight_line(NZL - 1)

    for p in range(PIECES - 1):
        res_first(0, p)
    attention_forward()
    weight_x2(0)
    weight_z(1)
    weight_z(2)
    code(0)
    weight_last(inner)
    weight_x2(1)
    cotangent_y()
    code_y(0)
    weight_last(outer)
    weight_x(3)
    res_z(0)
    weight_x2(2)
    res_z(1)
    cotangent_relay()
    res_first(0, 3)
    code_mid(0)
    res_second(0, 0)
    res_second(0, 1)
    res_core(0, 0, 0, 4)
    res_cores(0, 0, 2)
    code(1)
    code_y(1)
    weight_x2(3)
    res_second(0, 2)
    res_z(2)
    code(2)
    cotangent_c()
    grad_start(0)
    grad_start(1)
    code_mid(1)
    code_y(2)
    res_first(1, 0)
    code_z(0)
    res_z(3)
    code(3)
    code_y(3)
    res_second(0, 3)
    res_cores(0, 2, 2)
    grad_start(2)
    code_z(1)
    code_mid(2)
    res_first(1, 1)
    grad_on(0)
    res_core(0, 1, 0, 2)
    grad_start(3)
    grad_attn(0)
    grad_attn(1)
    grad_attn(2)
    grad_attn(3)
    res_last(0, 0, 2)
    res_first(1, 2)
    code_mid(3)
    grad_on(1)
    code_back(0)
    code_z(2)
    attention_backward()
    grad_on(2)
    grad_z(0)
    grad_on(3)
    res_first(1, 3)
    res_core(0, 1, 2, 2)
    code_z(3)
    code_back(1)
    code_out(0)
    grad_z(1)
    res_second(1, 0)
    res_second(1, 1)
    res_cores(1, 0, 2)
    res_last(0, 2, 2)
    code_back(2)
    grad_z(3)
    code_out(1)
    code_back(3)
    res_second(1, 2)
    grad_z(2)
    code_out(2)
    code_far(0)
    res_second(1, 3)
    res_cores(1, 2)
    code_out(3)
    code_far(1)
    res_last(1, 0)
    res_last(1, 1)
    res_cores(1, 3)
    code_far(2)
    code_far(3)
    res_last(1, 2)
    grad_end()
    res_last(1, 3)
    code_done()
    res_done()
    sends_done()


STEP_BLOCKS = 8
CLOSE_STEPS = NBLK // STEP_BLOCKS


def close_kernel(
    resid_ref, cs_ref, dec_ref, dq_in, dk_in, dv_in, gw_in,
    out_ref, dq_ref, dk_ref, dv_ref, gw_ref, layer, copy_sem, out_sem,
):
    copies = [
        pltpu.make_async_copy(src, dst, copy_sem.at[i])
        for i, (src, dst) in enumerate(
            ((dq_in, dq_ref), (dk_in, dk_ref), (dv_in, dv_ref), (gw_in, gw_ref))
        )
    ]
    for copy in copies:
        copy.start()
    depth, width = STEP_BLOCKS * CODE_W, STEP_BLOCKS * BLOCK
    per = CLOSE_STEPS // NZL
    row = lax.broadcasted_iota(jnp.int32, (depth, BLOCK), 0) // CODE_W
    for step in range(CLOSE_STEPS):
        cols = slice(step * width, (step + 1) * width)
        dec = dec_ref[step * depth : (step + 1) * depth, :]
        opened = jnp.concatenate(
            [jnp.where(row == b, dec, jnp.zeros_like(dec)) for b in range(STEP_BLOCKS)], axis=1
        )
        codes = cs_ref[step // per, :, (step % per) * depth : (step % per + 1) * depth]
        added = nn(codes, opened)
        for b in range(SEQ // TB):
            p = place(b)
            rows = slice(b * TB, (b + 1) * TB)
            layer[rows, cols] = (
                resid_ref[rows, cols].astype(F32) + added[p * TB : (p + 1) * TB]
            ).astype(BF)
        copies.append(
            pltpu.make_async_copy(layer.at[:, cols], out_ref.at[:, cols], out_sem.at[step])
        )
        copies[-1].start()
    for copy in copies:
        copy.wait()


def local(queries, key_rows, value_rows, residual_in, out_weight, encoder, decoder, grad_out):
    vmem = pl.BlockSpec(memory_space=pltpu.VMEM)
    anywhere = pl.BlockSpec(memory_space=pl.ANY)
    dec_rows = decoder.reshape(CODE, BLOCK)
    operands = (queries, key_rows, value_rows, residual_in, out_weight, encoder, dec_rows, grad_out)
    operands = [pltpu.with_memory_space_constraint(a, pltpu.HBM) for a in operands]
    resid, code_sum, dq, dk, dv, gw, dec_rows = pl.pallas_call(
        main_kernel,
        out_shape=(
            pltpu.VMEM((SEQ, D), BF),
            pltpu.VMEM((NZL, SEQ, CH), BF),
            pltpu.VMEM((SEQ, AW), BF),
            pltpu.VMEM((SEQ, AW), BF),
            pltpu.VMEM((SEQ, AW), BF),
            pltpu.VMEM((OWN * BLOCK, AW), F32),
            pltpu.VMEM((CODE, BLOCK), BF),
        ),
        in_specs=[anywhere] * 8,
        out_specs=(vmem,) * 7,
        scratch_shapes=[
            pltpu.VMEM((SEQ, AW), BF),
            pltpu.VMEM((SEQ, AW), BF),
            pltpu.VMEM((SEQ, AW), BF),
            pltpu.VMEM((OWN * BLOCK, AW), BF),
            pltpu.VMEM((OWN, CODE_W, BLOCK), BF),
            pltpu.VMEM((TB, D), BF),
            pltpu.VMEM((NZL, CH, AW), BF),
            pltpu.VMEM((NZL, SEQ, CH), BF),
            pltpu.VMEM((SEQ, AW), BF),
            pltpu.VMEM((HEADS, SEQ, SEQ), F32),
            pltpu.VMEM((SEQ, AW), F32),
            pltpu.VMEM((4, HALF, CH), BF),
            pltpu.VMEM((4, HALF, CH), BF),
            pltpu.VMEM((4, HALF, CH), BF),
            pltpu.VMEM((4, HALF, CH), BF),
            pltpu.VMEM((4, PAIR, CH), BF),
            pltpu.VMEM((4, PAIR, CH), BF),
            pltpu.VMEM((4, PAIR, CH), BF),
            pltpu.VMEM((4, PAIR, CH), BF),
            pltpu.VMEM((4, PAIR, CH), BF),
            pltpu.VMEM((4, PAIR, CH), BF),
            pltpu.VMEM((NZL, NX, ER, AW), BF),
            pltpu.VMEM((NZL, ER, AW), BF),
            pltpu.VMEM((NZL, ER, AW), BF),
            pltpu.VMEM((NZL, ER, AW), BF),
            pltpu.VMEM((NZL, ER, AW), BF),
            pltpu.VMEM((NZL, ER, AW), BF),
            pltpu.VMEM((3, ER, AW), BF),
            pltpu.VMEM((ER, AW), BF),
            pltpu.SemaphoreType.DMA((len(KINDS),)),
            pltpu.SemaphoreType.DMA((N_RECV,)),
            pltpu.SemaphoreType.DMA((5,)),
            pltpu.SemaphoreType.DMA((NZL,)),
            pltpu.SemaphoreType.DMA((NZL,)),
            pltpu.SemaphoreType.DMA((NZL,)),
            pltpu.SemaphoreType.DMA((8,)),
        ],
        name="exchange",
        compiler_params=pltpu.CompilerParams(
            collective_id=0, has_side_effects=True, vmem_limit_bytes=32 * 2**20
        ),
    )(*operands)

    return pl.pallas_call(
        close_kernel,
        out_shape=(
            pltpu.HBM((SEQ, D), BF),
            pltpu.HBM((SEQ, AW), BF),
            pltpu.HBM((SEQ, AW), BF),
            pltpu.HBM((SEQ, AW), BF),
            pltpu.HBM((OWN * BLOCK, AW), F32),
        ),
        in_specs=[vmem] * 7,
        out_specs=(anywhere,) * 5,
        scratch_shapes=[
            pltpu.VMEM((SEQ, D), BF),
            pltpu.SemaphoreType.DMA((4,)),
            pltpu.SemaphoreType.DMA((CLOSE_STEPS,)),
        ],
        name="close",
        compiler_params=pltpu.CompilerParams(vmem_limit_bytes=20 * 2**20),
    )(resid, code_sum, dec_rows, dq, dk, dv, gw)


def solution(mesh):
    placed = (
        P("dp", "tensor"),
        P("dp", "tensor"),
        P("dp", "tensor"),
        P(("dp", "tensor"), None),
        P("dp", "tensor"),
        P(),
        P(),
        P(("dp", "tensor"), None),
    )
    return jax.shard_map(
        local,
        mesh=mesh,
        in_specs=placed,
        out_specs=(
            P("dp", None),
            P("dp", "tensor"),
            P("dp", "tensor"),
            P("dp", "tensor"),
            P("dp", "tensor"),
        ),
        check_vma=False,
    )
```
